256 devices in a mesh: band: 32 (over z, x_hi, core), fft: 8 (over x_lo, y).
Axes of the slice: x: 4 (x_hi: 2, x_lo: 2; x = x_hi * 2 + x_lo), y: 4, z: 8, core: 2. Of those that a mesh axis runs over, the one named last changes fastest.
Arguments:
- orbitals: float32 [64, 64, 4096], P('band', 'fft'), may hold values from -6 to 6
Outputs:
- local_exchange: float32 [64, 64, 4096], P('band', 'fft')
- window_exchange: float32 [4, 64, 4096], P(None, 'fft')
The draws below stay inside these ranges and needn't reach their ends.
All inputs are finite; a program needn't handle non-finite values.
Results may differ from the reference program's by a relative error of at most 0.00019.
Values sent between devices are 32-bit elements; how exact they have to be, the bound alone decides.
A program may use at most 64 MiB of HBM per device.

```python
import math
import jax
import jax.numpy as jnp
from jax import lax

GRID = 64
ORB_DEV = 2
TOTAL = 64
N_BAND = 32


def shard_levels(stream_key, shape, shards, low, high):
    def one(position, blocks):
        steps = jax.random.uniform(jax.random.fold_in(jax.random.fold_in(stream_key, 6), position), (blocks,), jnp.float32, low / len(shards), high / len(shards))
        return jnp.repeat(jnp.exp(steps), shape[position] // blocks).reshape((-1,) + (1,) * (len(shape) - position - 1))

    gain = one(*shards[0])
    for cut in shards[1:]:
        gain = gain * one(*cut)
    return gain


def scatter_about(key, shape, spread, reach, cuts=(), kind=jnp.bfloat16):
    drawn = jax.random.normal(key, shape, jnp.float32) * spread
    if len(cuts) > 0:
        drawn = shard_levels(key, shape, cuts, -0.22, 0.18) * drawn
    return jnp.clip(drawn, min=-reach, max=reach).astype(kind)


def setup_inputs(seed: int = 0) -> dict:
    splits = jax.random.split(jax.random.key(seed), 2)
    orbitals = scatter_about(splits[0], (TOTAL, GRID, GRID * GRID), 1.0, 6.0, ((0, 32), (1, 8)), jnp.float32)
    return dict(orbitals=orbitals)


spacing = 0.367
mixing = 0.25


def folded(values, extent):
    return jnp.where(2 * values < extent, values, values - extent)


def coulomb(kx_index, ky_index, kz_index, extent):
    squared = folded(kx_index, extent) ** 2 + folded(ky_index, extent) ** 2 + folded(kz_index, extent) ** 2
    factor = (2.0 * math.pi / (extent * spacing)) ** 2
    clamped = jnp.maximum(squared, 1).astype(jnp.float32)
    return jnp.where(squared > 0, (4.0 * math.pi / factor) / clamped, jnp.float32(0.0)).astype(jnp.float32)


def reference(orbitals):
    orbital_total = orbitals.shape[0]
    orbital_grids = orbitals.reshape(orbital_total, GRID, GRID, GRID)
    second_root = (N_BAND // 2) * ORB_DEV
    window = jnp.concatenate([orbital_grids[:ORB_DEV], orbital_grids[second_root:second_root + ORB_DEV]], 0)
    spans = jnp.arange(GRID, dtype=jnp.int32)
    kernel = coulomb(spans[:, None, None], spans[None, :, None], spans[None, None, :], GRID)

    def advance(state, own_orbital):
        density = own_orbital[None] * window
        spectrum = jnp.fft.fftn(density, axes=(1, 2, 3)) * kernel
        potential = jnp.real(jnp.fft.ifftn(spectrum, axes=(1, 2, 3)))
        local_term = -mixing * jnp.sum(window * potential, 0)
        return state - mixing * own_orbital[None] * potential, local_term

    window_total, local_terms = lax.scan(advance, jnp.zeros_like(window), orbital_grids)
    return (local_terms.reshape(orbital_total, GRID, GRID * GRID),
            window_total.reshape(2 * ORB_DEV, GRID, GRID * GRID))
```

```python
import functools
import math

import jax
import jax.numpy as jnp
import ml_dtypes
import numpy as np
from jax import lax
from jax.experimental import pallas as pl
from jax.experimental.pallas import tpu as pltpu
from jax.sharding import PartitionSpec as P

GRID = 64
LANES = 128
PLANES = 8
HALF = 32
SPACING = 0.367
MIXING = 0.25
MESH = pl.DeviceIdType.MESH
BF16 = jnp.bfloat16
F32 = jnp.float32
UNROLL = 2


def split_table(table):
    high = table.astype(ml_dtypes.bfloat16)
    low = (table - high.astype(np.float64)).astype(ml_dtypes.bfloat16)
    return high, low


def make_tables():
    counter = np.arange(GRID)
    angles = (counter[:, None] * counter[None, :] % GRID) * (2.0 * np.pi / GRID)
    cosine, sine = np.cos(angles), np.sin(angles)
    depth = []
    for sign in (1.0, -1.0):
        table = np.block([[cosine, -sign * sine], [sign * sine, cosine]])
        high, low = split_table(table)
        row = np.concatenate([high, low], 1)
        depth.append(np.concatenate([row, row], 0))
    order = np.concatenate([np.arange(0, GRID, 2), np.arange(1, GRID, 2)])

    def stacked(rows, columns):
        table = np.concatenate(
            [cosine[np.ix_(rows, columns)], sine[np.ix_(rows, columns)]], 0
        )
        high, low = split_table(table)
        return np.concatenate([high, low, high, low], 1)

    return depth + [
        stacked(counter, order),
        stacked(counter, counter),
        stacked(order, counter),
    ]


def split_values(values):
    high = values.astype(BF16)
    low = (values - high.astype(F32)).astype(BF16)
    return high, low


def along_lanes(values, table):
    high, low = split_values(values)
    both = jnp.dot(jnp.concatenate([high, low], 1), table, preferred_element_type=F32)
    return both[:, :LANES] + both[:, LANES:]


def along_rows(first, second, table, sign):
    high, low = split_values(jnp.concatenate([first, second], 1))
    stack = jnp.concatenate([high, high, low, low], 0)
    both = jnp.dot(table, stack, preferred_element_type=F32)
    outs = []
    for index in range(2):
        columns = slice(index * LANES, (index + 1) * LANES)
        cos_part, sin_part = both[:GRID, columns], both[GRID:, columns]
        outs.append(cos_part + sign * pltpu.roll(sin_part, GRID, 1))
    return outs


def wait_for(ref, sem):
    pltpu.make_async_copy(ref, ref, sem).wait()


def kernel(
    nf, nq,
    orb_ref, fz_ref, iz_ref, fy_ref, fx_ref, iy_ref,
    local_ref, window_ref,
    obuf, dbuf, ktab, wbuf, fsend, frecv, bsend, brecv, part, pbuf, hbuf, rsbuf, acc, fin,
    sc_s, sc_r, ag_s, ag_r, cx_s, cx_r, f_s, f_r, b_s, b_r,
    p_s, p_r, rs_s, rs_r, ga_s, ga_r, fx_s, fx_r,
):
    band = lax.axis_index("band")
    me = lax.axis_index("fft")
    core = lax.rem(band, 2)
    chip = band // 2
    other = band + 1 - 2 * core
    second_root = nq
    root_chip = second_root // 2
    rows = 256 // nq

    barrier = pltpu.get_barrier_semaphore()

    def signal(b, f):
        pl.semaphore_signal(barrier, inc=1, device_id=(b, f), device_id_type=MESH)

    def greet_fft(step, carry):
        signal(band, lax.rem(me + step, nf))
        return carry

    def greet_band(step, carry):
        signal(2 * lax.rem(chip + step, nq) + core, me)
        return carry

    lax.fori_loop(1, nf, greet_fft, 0)
    lax.fori_loop(1, nq, greet_band, 0)
    signal(other, me)

    @pl.when(jnp.logical_and(core == 1, chip != root_chip))
    def _():
        signal(second_root, me)

    @pl.when(band == second_root)
    def _():
        def greet_odd(step, carry):
            signal(2 * lax.rem(chip + step, nq) + 1, me)
            return carry

        lax.fori_loop(1, nq, greet_odd, 0)

    extra = jnp.where(
        band == second_root, nq - 1, jnp.where(jnp.logical_and(core == 1, chip != root_chip), 1, 0)
    )
    pl.semaphore_wait(barrier, nf - 1 + nq - 1 + 1 + extra)

    @pl.when(band == 0)
    def _():
        pltpu.make_async_copy(
            orb_ref.at[:, pl.ds(0, rows), :], wbuf.at[pl.ds(0, 2), pl.ds(0, rows), :], sc_r
        ).start()

        def scatter(p, carry):
            piece = pl.ds(pl.multiple_of(p * rows, rows), rows)
            pltpu.make_async_remote_copy(
                orb_ref.at[:, piece, :], wbuf.at[pl.ds(0, 2), piece, :], sc_s, sc_r,
                device_id=(2 * p, me), device_id_type=MESH,
            ).start()
            return carry

        lax.fori_loop(1, nq, scatter, 0)

    @pl.when(band == second_root)
    def _():
        def scatter(p, carry):
            piece = pl.ds(pl.multiple_of(p * rows, rows), rows)
            pltpu.make_async_remote_copy(
                orb_ref.at[:, piece, :], wbuf.at[pl.ds(2, 2), piece, :], sc_s, sc_r,
                device_id=(2 * p + 1, me), device_id_type=MESH,
            ).start()
            return carry

        lax.fori_loop(0, nq, scatter, 0)

    lane = lax.broadcasted_iota(jnp.int32, (GRID, LANES), 1)
    low_lane = lane < GRID
    sign = jnp.where(low_lane, 1.0, -1.0).astype(F32)

    def fold(values):
        return jnp.where(2 * values < GRID, values, values - GRID)

    kz = fold(jnp.where(low_lane, lane, lane - GRID))
    kx = fold(lax.broadcasted_iota(jnp.int32, (GRID, LANES), 0))
    base = kx * kx + kz * kz
    factor = (2.0 * math.pi / (GRID * SPACING)) ** 2
    scale = -MIXING / GRID**3

    for row in range(GRID // nf):
        ky = fold(me * (GRID // nf) + row)
        squared = base + ky * ky
        clamped = jnp.maximum(squared, 1).astype(F32)
        ktab[row] = jnp.where(
            squared > 0, (4.0 * math.pi / factor * scale) / clamped, 0.0
        )

    half_lane = low_lane[:HALF]

    def pack_orbitals(x, carry):
        source = pl.ds(pl.multiple_of(x * HALF, HALF), HALF)
        first, second = orb_ref[0, source, :], orb_ref[1, source, :]
        start = pl.multiple_of(x * GRID, GRID)
        obuf[pl.ds(start, HALF), :] = jnp.where(half_lane, first, pltpu.roll(second, GRID, 1))
        obuf[pl.ds(start + HALF, HALF), :] = jnp.where(
            half_lane, pltpu.roll(first, GRID, 1), second
        )
        return carry

    lax.fori_loop(0, PLANES, pack_orbitals, 0)

    mine = pl.ds(2 * core, 2)
    wait_for(wbuf.at[pl.ds(0, 2), pl.ds(0, rows), :], sc_r)
    own_piece = pl.ds(pl.multiple_of(chip * rows, rows), rows)

    def gather(step, carry):
        p = lax.rem(chip + step, nq)
        pltpu.make_async_remote_copy(
            wbuf.at[mine, own_piece, :], wbuf.at[mine, own_piece, :], ag_s, ag_r,
            device_id=(2 * p + core, me), device_id_type=MESH,
        ).start()
        return carry

    lax.fori_loop(1, nq, gather, 0)
    wait_for(wbuf.at[pl.ds(0, 2), pl.ds(0, (nq - 1) * rows), :], ag_r)
    cross = pltpu.make_async_remote_copy(
        wbuf.at[mine], wbuf.at[mine], cx_s, cx_r, device_id=(other, me), device_id_type=MESH
    )
    cross.start()

    block = GRID * PLANES // nf

    def exchange(source, target, send_sem, recv_sem, k):
        own = pl.ds(pl.multiple_of(me * block, block), block)
        pltpu.make_async_copy(source.at[k, own, :], target.at[k, me], recv_sem.at[k]).start()

        def send(step, carry):
            p = lax.rem(me + step, nf)
            pltpu.make_async_remote_copy(
                source.at[k, pl.ds(pl.multiple_of(p * block, block), block), :],
                target.at[k, me], send_sem.at[k], recv_sem.at[k],
                device_id=(band, p), device_id_type=MESH,
            ).start()
            return carry

        lax.fori_loop(1, nf, send, 0)

    def forward(k):
        j = lax.rem(2 * core + k, 4)

        def step(i, carry):
            for inner in range(2):
                x = 2 * i + inner
                values = wbuf[j, pl.ds(pl.multiple_of(x * HALF, HALF), HALF), :]
                turned = pltpu.roll(values, GRID, 1)
                start = pl.multiple_of(x * GRID, GRID)
                dbuf[k, pl.ds(start, HALF), :] = jnp.where(half_lane, values, turned)
                dbuf[k, pl.ds(start + HALF, HALF), :] = jnp.where(half_lane, turned, values)
            both = pl.ds(pl.multiple_of(i * 2 * GRID, 2 * GRID), 2 * GRID)
            field = along_lanes(obuf[both, :] * dbuf[k, both, :], fz_ref[...])
            outs = along_rows(field[:GRID], field[GRID:], fy_ref[...], sign)
            for inner in range(2):
                fsend[k, pl.ds(2 * i + inner, GRID, stride=PLANES), :] = outs[inner]
            return carry

        lax.fori_loop(0, PLANES // 2, step, 0, unroll=UNROLL)
        exchange(fsend, frecv, f_s, f_r, k)

    def middle(k):
        wait_for(frecv.at[k], f_r.at[k])

        def step(i, carry):
            pair = []
            for inner in range(2):
                start = pl.multiple_of((2 * i + inner) * PLANES, PLANES)
                pair.append(frecv[k, :, pl.ds(start, PLANES), :].reshape(GRID, LANES))
            outs = along_rows(pair[0], pair[1], fx_ref[...], sign)
            outs = [outs[inner] * ktab[2 * i + inner] for inner in range(2)]
            outs = along_rows(outs[0], outs[1], fx_ref[...], -sign)
            for inner in range(2):
                bsend[k, pl.ds(2 * i + inner, GRID, stride=PLANES), :] = outs[inner]
            return carry

        lax.fori_loop(0, GRID // nf // 2, step, 0, unroll=UNROLL)
        exchange(bsend, brecv, b_s, b_r, k)

    def backward(k):
        wait_for(brecv.at[k], b_r.at[k])

        def step(i, carry):
            pair = []
            for inner in range(2):
                start = pl.multiple_of((2 * i + inner) * PLANES, PLANES)
                pair.append(brecv[k, :, pl.ds(start, PLANES), :].reshape(GRID, LANES))
            outs = along_rows(pair[0], pair[1], iy_ref[...], -sign)
            potential = along_lanes(jnp.concatenate(outs, 0), iz_ref[...])
            both = pl.ds(pl.multiple_of(i * 2 * GRID, 2 * GRID), 2 * GRID)
            term = dbuf[k, both, :] * potential
            if k == 0:
                acc[both, :] = term
            else:
                acc[both, :] += term
            product = obuf[both, :] * potential
            total = product + pltpu.roll(product, GRID, 1)
            for inner in range(2):
                start = inner * GRID
                part[k, pl.ds(pl.multiple_of((2 * i + inner) * HALF, HALF), HALF), :] = jnp.where(
                    half_lane, total[start:start + HALF], total[start + HALF:start + GRID]
                )
            return carry

        lax.fori_loop(0, PLANES // 2, step, 0, unroll=UNROLL)

    def to_partner(source, target, send_sem, recv_sem):
        pltpu.make_async_remote_copy(
            source, target, send_sem, recv_sem, device_id=(other, me), device_id_type=MESH
        ).start()

    def scatter_sum(k):
        wait_for(pbuf.at[k], p_r.at[k])
        hbuf[k] = part[k + 2] + pbuf[k]
        rsbuf[k, chip] = hbuf[k, own_piece, :]

        def send(step, carry):
            p = lax.rem(chip + step, nq)
            pltpu.make_async_remote_copy(
                hbuf.at[k, pl.ds(pl.multiple_of(p * rows, rows), rows), :], rsbuf.at[k, chip],
                rs_s.at[k], rs_r.at[k], device_id=(2 * p + core, me), device_id_type=MESH,
            ).start()
            return carry

        lax.fori_loop(1, nq, send, 0)

    theirs = 2 - 2 * core

    def gather_sum(k):
        wait_for(rsbuf.at[k, pl.ds(0, nq - 1)], rs_r.at[k])
        total = rsbuf[k, 0]
        for slot in range(1, nq):
            total = total + rsbuf[k, slot]
        fin[theirs + k, own_piece, :] = total

        def send(step, carry):
            p = lax.rem(chip + step, nq)
            pltpu.make_async_remote_copy(
                fin.at[theirs + k, own_piece, :], fin.at[theirs + k, own_piece, :],
                ga_s.at[k], ga_r.at[k], device_id=(2 * p + core, me), device_id_type=MESH,
            ).start()
            return carry

        lax.fori_loop(1, nq, send, 0)

    def share_sum(k):
        wait_for(fin.at[k, pl.ds(0, (nq - 1) * rows), :], ga_r.at[k])
        to_partner(fin.at[theirs + k], fin.at[theirs + k], fx_s.at[k], fx_r.at[k])

    forward(0)
    forward(1)
    wait_for(wbuf.at[pl.ds(0, 2)], cx_r)
    forward(2)
    forward(3)
    for k in range(4):
        middle(k)
    for k in range(2):
        backward(k)
        to_partner(part.at[k], pbuf.at[k], p_s.at[k], p_r.at[k])
    for k in range(2):
        backward(k + 2)
        scatter_sum(k)

    def unpack(x, carry):
        start = pl.multiple_of(x * GRID, GRID)
        even, odd = acc[pl.ds(start, HALF), :], acc[pl.ds(start + HALF, HALF), :]
        target = pl.ds(pl.multiple_of(x * HALF, HALF), HALF)
        local_ref[0, target, :] = jnp.where(half_lane, even, pltpu.roll(odd, GRID, 1))
        local_ref[1, target, :] = jnp.where(half_lane, pltpu.roll(even, GRID, 1), odd)
        return carry

    lax.fori_loop(0, PLANES, unpack, 0)
    for k in range(2):
        gather_sum(k)
    for k in range(2):
        share_sum(k)

    @pl.when(band == 0)
    def _():
        wait_for(wbuf.at[pl.ds(0, 2), pl.ds(0, (nq - 1) * rows), :], sc_s)

    @pl.when(band == second_root)
    def _():
        wait_for(wbuf.at[pl.ds(0, 2)], sc_s)

    wait_for(wbuf.at[pl.ds(0, 2), pl.ds(0, (nq - 1) * rows), :], ag_s)
    wait_for(wbuf.at[pl.ds(0, 2)], cx_s)
    for k in range(4):
        wait_for(frecv.at[k, pl.ds(0, nf - 1)], f_s.at[k])
        wait_for(brecv.at[k, pl.ds(0, nf - 1)], b_s.at[k])
    for k in range(2):
        wait_for(pbuf.at[k], p_s.at[k])
        wait_for(rsbuf.at[k, pl.ds(0, nq - 1)], rs_s.at[k])
        wait_for(fin.at[k, pl.ds(0, (nq - 1) * rows), :], ga_s.at[k])
        wait_for(fin.at[k], fx_s.at[k])
        wait_for(fin.at[k], fx_r.at[k])
    window_ref[...] = fin[...]


def body(orbitals):
    nf = lax.axis_size("fft")
    nq = lax.axis_size("band") // 2
    rows = 256 // nq
    block = GRID * PLANES // nf
    tables = [jnp.asarray(table) for table in make_tables()]
    dma, vmem = pltpu.SemaphoreType.DMA, pltpu.VMEM
    local_out, window_out = pl.pallas_call(
        functools.partial(kernel, nf, nq),
        out_shape=(
            jax.ShapeDtypeStruct((2, PLANES * HALF, LANES), F32),
            jax.ShapeDtypeStruct((4, PLANES * HALF, LANES), F32),
        ),
        in_specs=[pl.BlockSpec(memory_space=vmem)] * 6,
        out_specs=(pl.BlockSpec(memory_space=vmem),) * 2,
        scratch_shapes=[
            vmem((PLANES * GRID, LANES), F32),
            vmem((4, PLANES * GRID, LANES), F32),
            vmem((GRID // nf, GRID, LANES), F32),
            vmem((4, 256, LANES), F32),
            vmem((4, PLANES * GRID, LANES), F32),
            vmem((4, nf, block, LANES), F32),
            vmem((4, PLANES * GRID, LANES), F32),
            vmem((4, nf, block, LANES), F32),
            vmem((4, 256, LANES), F32),
            vmem((2, 256, LANES), F32),
            vmem((2, 256, LANES), F32),
            vmem((2, nq, rows, LANES), F32),
            vmem((PLANES * GRID, LANES), F32),
            vmem((4, 256, LANES), F32),
            dma, dma, dma, dma, dma, dma,
            dma((4,)), dma((4,)), dma((4,)), dma((4,)),
            dma((2,)), dma((2,)), dma((2,)), dma((2,)),
            dma((2,)), dma((2,)), dma((2,)), dma((2,)),
        ],
        compiler_params=pltpu.CompilerParams(
            collective_id=0, has_side_effects=True, vmem_limit_bytes=40 * 1024 * 1024
        ),
        cost_estimate=pl.CostEstimate(
            flops=6 * 4 * 2 * 512 * 256 * 256, bytes_accessed=1 << 20, transcendentals=0
        ),
    )(orbitals.reshape(2, PLANES * HALF, LANES), *tables)
    return (
        local_out.reshape(2, PLANES, GRID * GRID),
        window_out.reshape(4, PLANES, GRID * GRID),
    )


def solution(mesh):
    return jax.shard_map(
        body,
        mesh=mesh,
        in_specs=(P("band", "fft", None),),
        out_specs=(P("band", "fft", None), P(None, "fft", None)),
        check_vma=False,
    )
```

```python
import functools
import math

import jax
import jax.numpy as jnp
import ml_dtypes
import numpy as np
from jax import lax
from jax.experimental import pallas as pl
from jax.experimental.pallas import tpu as pltpu
from jax.sharding import PartitionSpec as P

GRID = 64
LANES = 128
PLANES = 8
HALF = 32
SPACING = 0.367
MIXING = 0.25
MESH = pl.DeviceIdType.MESH
BF16 = jnp.bfloat16
F32 = jnp.float32


def split_table(table):
    high = table.astype(ml_dtypes.bfloat16)
    low = (table - high.astype(np.float64)).astype(ml_dtypes.bfloat16)
    return high, low


def make_tables():
    counter = np.arange(GRID)
    angles = (counter[:, None] * counter[None, :] % GRID) * (2.0 * np.pi / GRID)
    cosine, sine = np.cos(angles), np.sin(angles)
    depth = []
    for sign in (1.0, -1.0):
        table = np.block([[cosine, -sign * sine], [sign * sine, cosine]])
        high, low = split_table(table)
        row = np.concatenate([high, low], 1)
        depth.append(np.concatenate([row, row], 0))
    order = np.concatenate([np.arange(0, GRID, 2), np.arange(1, GRID, 2)])

    def stacked(rows, columns):
        table = np.concatenate(
            [cosine[np.ix_(rows, columns)], sine[np.ix_(rows, columns)]], 0
        )
        high, low = split_table(table)
        return np.concatenate([high, low, high, low], 1)

    return depth + [
        stacked(counter, order),
        stacked(counter, counter),
        stacked(order, counter),
    ]


def split_values(values):
    high = values.astype(BF16)
    low = (values - high.astype(F32)).astype(BF16)
    return high, low


def along_lanes(values, table):
    high, low = split_values(values)
    both = jnp.dot(jnp.concatenate([high, low], 1), table, preferred_element_type=F32)
    return both[:, :LANES] + both[:, LANES:]


def along_rows(first, second, table, sign):
    high, low = split_values(jnp.concatenate([first, second], 1))
    stack = jnp.concatenate([high, high, low, low], 0)
    both = jnp.dot(table, stack, preferred_element_type=F32)
    outs = []
    for index in range(2):
        columns = slice(index * LANES, (index + 1) * LANES)
        cos_part, sin_part = both[:GRID, columns], both[GRID:, columns]
        outs.append(cos_part + sign * pltpu.roll(sin_part, GRID, 1))
    return outs


def loop(first, last, step):
    def advance(index, carry):
        step(index)
        return carry

    lax.fori_loop(first, last, advance, 0, unroll=last - first)


def wait_for(ref, sem):
    pltpu.make_async_copy(ref, ref, sem).wait()


def kernel(
    nf, nq,
    orb_hbm, fz_hbm, iz_hbm, fy_hbm, fx_hbm, iy_hbm,
    local_ref, window_ref,
    orb, fz, iz, fy, fx, iy,
    obuf, dbuf, ktab, wbuf, fsend, frecv, bsend, brecv, part, pbuf, hbuf, rsbuf, acc, fin,
    in_sem, table_sem, sc_s, sc_r, ag_s, ag_r, cx_s, cx_r, f_s, f_r, b_s, b_r,
    p_s, p_r, rs_s, rs_r, ga_s, ga_r, fx_s, fx_r,
):
    band = lax.axis_index("band")
    me = lax.axis_index("fft")
    core = lax.rem(band, 2)
    chip = band // 2
    other = band + 1 - 2 * core
    second_root = nq
    root_chip = second_root // 2
    rows = 256 // nq
    columns = 2
    levels = nq // columns
    level, column = chip // columns, lax.rem(chip, columns)
    width = GRID * GRID // levels

    barrier = pltpu.get_barrier_semaphore()

    def signal(b, f):
        pl.semaphore_signal(barrier, inc=1, device_id=(b, f), device_id_type=MESH)

    @pl.when(jnp.logical_and(core == 1, chip != root_chip))
    def _():
        signal(second_root, me)

    loop(1, nq, lambda step: signal(2 * lax.rem(chip + step, nq) + core, me))
    loop(1, nf, lambda step: signal(band, lax.rem(me + step, nf)))
    signal(other, me)

    @pl.when(band == second_root)
    def _():
        loop(1, nq, lambda step: signal(2 * lax.rem(chip + step, nq) + 1, me))

    loads = [pltpu.make_async_copy(orb_hbm, orb, in_sem)]
    loads += [
        pltpu.make_async_copy(source, target, table_sem.at[index])
        for index, (source, target) in enumerate(
            ((fz_hbm, fz), (iz_hbm, iz), (fy_hbm, fy), (fx_hbm, fx), (iy_hbm, iy))
        )
    ]
    for load in loads:
        load.start()
    loads[0].wait()

    extra = jnp.where(
        band == second_root, nq - 1, jnp.where(jnp.logical_and(core == 1, chip != root_chip), 1, 0)
    )
    pl.semaphore_wait(barrier, nf - 1 + nq - 1 + 1 + extra)

    def span(place):
        return pl.ds(pl.multiple_of(place * width, width), width)

    def scatter(window, root, p):
        piece = span(p // columns)
        pltpu.make_async_remote_copy(
            orb.at[window, :, piece], wbuf.at[2 * root + window, :, piece],
            sc_s.at[window], sc_r.at[window],
            device_id=(2 * p + root, me), device_id_type=MESH,
        ).start()

    @pl.when(band == 0)
    def _():
        for window in range(2):
            pltpu.make_async_copy(
                orb.at[window, :, pl.ds(0, width)], wbuf.at[window, :, pl.ds(0, width)],
                sc_r.at[window],
            ).start()
            loop(1, nq, lambda p: scatter(window, 0, p))

    @pl.when(band == second_root)
    def _():
        for window in range(2):
            loop(0, nq, lambda p: scatter(window, 1, p))

    lane = lax.broadcasted_iota(jnp.int32, (GRID, LANES), 1)
    low_lane = lane < GRID
    sign = jnp.where(low_lane, 1.0, -1.0).astype(F32)

    def fold(values):
        return jnp.where(2 * values < GRID, values, values - GRID)

    kz = fold(jnp.where(low_lane, lane, lane - GRID))
    kx = fold(lax.broadcasted_iota(jnp.int32, (GRID, LANES), 0))
    base = kx * kx + kz * kz
    factor = (2.0 * math.pi / (GRID * SPACING)) ** 2
    scale = -MIXING / GRID**3

    for row in range(GRID // nf):
        ky = fold(me * (GRID // nf) + row)
        squared = base + ky * ky
        clamped = jnp.maximum(squared, 1).astype(F32)
        ktab[row] = jnp.where(
            squared > 0, (4.0 * math.pi / factor * scale) / clamped, 0.0
        )

    tile_lane, half_lane = low_lane[:PLANES], low_lane[:HALF]

    def tile(t):
        return pl.ds(pl.multiple_of(t * LANES, LANES), LANES)

    def pack_orbitals(t):
        first, second = orb[0, :, tile(t)], orb[1, :, tile(t)]
        obuf[pl.ds(t, PLANES, stride=GRID), :] = jnp.where(
            tile_lane, first, pltpu.roll(second, GRID, 1)
        )
        obuf[pl.ds(t + HALF, PLANES, stride=GRID), :] = jnp.where(
            tile_lane, pltpu.roll(first, GRID, 1), second
        )

    loop(0, HALF, pack_orbitals)
    for load in loads[1:]:
        load.wait()

    def gather(window):
        mine = wbuf.at[2 * core + window, :, span(level)]
        wait_for(wbuf.at[window, :, pl.ds(0, width)], sc_r.at[window])

        def send(step):
            p = lax.rem(level + step, levels) * columns + column
            pltpu.make_async_remote_copy(
                mine, mine, ag_s.at[window], ag_r.at[window],
                device_id=(2 * p + core, me), device_id_type=MESH,
            ).start()

        loop(1, levels, send)

    def cross(window):
        wait_for(wbuf.at[window, :, pl.ds(0, (levels - 1) * width)], ag_r.at[window])
        whole = wbuf.at[2 * core + window]
        pltpu.make_async_remote_copy(
            whole, whole, cx_s.at[window], cx_r.at[window],
            device_id=(other, me), device_id_type=MESH,
        ).start()

    block = GRID * PLANES // nf

    def exchange(source, target, send_sem, recv_sem, k):
        own = pl.ds(pl.multiple_of(me * block, block), block)
        pltpu.make_async_copy(source.at[k, own, :], target.at[k, me], recv_sem.at[k]).start()

        def send(step):
            p = lax.rem(me + step, nf)
            pltpu.make_async_remote_copy(
                source.at[k, pl.ds(pl.multiple_of(p * block, block), block), :],
                target.at[k, me], send_sem.at[k], recv_sem.at[k],
                device_id=(band, p), device_id_type=MESH,
            ).start()

        loop(1, nf, send)

    def forward(k):
        j = lax.rem(2 * core + k, 4)

        def widen(t):
            values = wbuf[j, :, tile(t)]
            turned = pltpu.roll(values, GRID, 1)
            dbuf[k, pl.ds(t, PLANES, stride=GRID), :] = jnp.where(tile_lane, values, turned)
            dbuf[k, pl.ds(t + HALF, PLANES, stride=GRID), :] = jnp.where(
                tile_lane, turned, values
            )

        loop(0, HALF, widen)

        def step(i):
            both = pl.ds(pl.multiple_of(i * 2 * GRID, 2 * GRID), 2 * GRID)
            field = along_lanes(obuf[both, :] * dbuf[k, both, :], fz[...])
            outs = along_rows(field[:GRID], field[GRID:], fy[...], sign)
            for inner in range(2):
                fsend[k, pl.ds(2 * i + inner, GRID, stride=PLANES), :] = outs[inner]

        loop(0, PLANES // 2, step)
        exchange(fsend, frecv, f_s, f_r, k)

    def middle(k):
        wait_for(frecv.at[k], f_r.at[k])

        def step(i):
            pair = []
            for inner in range(2):
                start = pl.multiple_of((2 * i + inner) * PLANES, PLANES)
                pair.append(frecv[k, :, pl.ds(start, PLANES), :].reshape(GRID, LANES))
            outs = along_rows(pair[0], pair[1], fx[...], sign)
            outs = [outs[inner] * ktab[2 * i + inner] for inner in range(2)]
            outs = along_rows(outs[0], outs[1], fx[...], -sign)
            for inner in range(2):
                bsend[k, pl.ds(2 * i + inner, GRID, stride=PLANES), :] = outs[inner]

        loop(0, GRID // nf // 2, step)
        exchange(bsend, brecv, b_s, b_r, k)

    def backward(k):
        wait_for(brecv.at[k], b_r.at[k])

        def step(i):
            pair = []
            for inner in range(2):
                start = pl.multiple_of((2 * i + inner) * PLANES, PLANES)
                pair.append(brecv[k, :, pl.ds(start, PLANES), :].reshape(GRID, LANES))
            outs = along_rows(pair[0], pair[1], iy[...], -sign)
            potential = along_lanes(jnp.concatenate(outs, 0), iz[...])
            both = pl.ds(pl.multiple_of(i * 2 * GRID, 2 * GRID), 2 * GRID)
            term = dbuf[k, both, :] * potential
            if k == 0:
                acc[both, :] = term
            else:
                acc[both, :] += term
            product = obuf[both, :] * potential
            total = product + pltpu.roll(product, GRID, 1)
            for inner in range(2):
                start = inner * GRID
                part[k, pl.ds(2 * i + inner, HALF, stride=PLANES), :] = jnp.where(
                    half_lane, total[start:start + HALF], total[start + HALF:start + GRID]
                )

        loop(0, PLANES // 2, step)

    own_piece = pl.ds(pl.multiple_of(chip * rows, rows), rows)

    def to_partner(source, target, send_sem, recv_sem):
        pltpu.make_async_remote_copy(
            source, target, send_sem, recv_sem, device_id=(other, me), device_id_type=MESH
        ).start()

    def scatter_sum(k):
        wait_for(pbuf.at[k], p_r.at[k])
        hbuf[k] = part[k + 2] + pbuf[k]
        rsbuf[k, chip] = hbuf[k, own_piece, :]

        def send(step):
            p = lax.rem(chip + step, nq)
            pltpu.make_async_remote_copy(
                hbuf.at[k, pl.ds(pl.multiple_of(p * rows, rows), rows), :], rsbuf.at[k, chip],
                rs_s.at[k], rs_r.at[k], device_id=(2 * p + core, me), device_id_type=MESH,
            ).start()

        loop(1, nq, send)

    theirs = 2 - 2 * core

    def gather_sum(k):
        wait_for(rsbuf.at[k, pl.ds(0, nq - 1)], rs_r.at[k])
        total = rsbuf[k, 0]
        for slot in range(1, nq):
            total = total + rsbuf[k, slot]
        fin[theirs + k, own_piece, :] = total

        def send(step):
            p = lax.rem(chip + step, nq)
            pltpu.make_async_remote_copy(
                fin.at[theirs + k, own_piece, :], fin.at[theirs + k, own_piece, :],
                ga_s.at[k], ga_r.at[k], device_id=(2 * p + core, me), device_id_type=MESH,
            ).start()

        loop(1, nq, send)

    def share_sum(k):
        wait_for(fin.at[k, pl.ds(0, (nq - 1) * rows), :], ga_r.at[k])
        to_partner(fin.at[theirs + k], fin.at[theirs + k], fx_s.at[k], fx_r.at[k])

    def write_window(j, t):
        start = pl.multiple_of(t * PLANES, PLANES)
        window_ref[j, :, tile(t)] = fin[j, pl.ds(start, PLANES), :]

    gather(0)
    gather(1)
    for window in range(2):
        cross(window)
        forward(window)
    for window in range(2):
        wait_for(wbuf.at[window], cx_r.at[window])
        forward(window + 2)
    for k in range(4):
        middle(k)
    for k in range(2):
        backward(k)
        to_partner(part.at[k], pbuf.at[k], p_s.at[k], p_r.at[k])
    for k in range(2):
        backward(k + 2)
        scatter_sum(k)

    def unpack(t):
        even = acc[pl.ds(t, PLANES, stride=GRID), :]
        odd = acc[pl.ds(t + HALF, PLANES, stride=GRID), :]
        local_ref[0, :, tile(t)] = jnp.where(tile_lane, even, pltpu.roll(odd, GRID, 1))
        local_ref[1, :, tile(t)] = jnp.where(tile_lane, pltpu.roll(even, GRID, 1), odd)

    loop(0, HALF, unpack)
    for k in range(2):
        gather_sum(k)
    for k in range(2):
        share_sum(k)

    @pl.when(band == 0)
    def _():
        for window in range(2):
            sent = (nq - 1) * PLANES * width // LANES
            wait_for(fsend.at[0, pl.ds(0, sent), :], sc_s.at[window])

    @pl.when(band == second_root)
    def _():
        for window in range(2):
            sent = nq * PLANES * width // LANES
            wait_for(fsend.at[0, pl.ds(0, sent), :], sc_s.at[window])

    for window in range(2):
        wait_for(wbuf.at[window, :, pl.ds(0, (levels - 1) * width)], ag_s.at[window])
        wait_for(wbuf.at[window], cx_s.at[window])
    for k in range(4):
        wait_for(frecv.at[k, pl.ds(0, nf - 1)], f_s.at[k])
        wait_for(brecv.at[k, pl.ds(0, nf - 1)], b_s.at[k])
    for k in range(2):
        wait_for(pbuf.at[k], p_s.at[k])
        wait_for(rsbuf.at[k, pl.ds(0, nq - 1)], rs_s.at[k])
        wait_for(fin.at[k, pl.ds(0, (nq - 1) * rows), :], ga_s.at[k])
        wait_for(fin.at[k], fx_s.at[k])
        wait_for(fin.at[k], fx_r.at[k])
    for j in range(4):
        loop(0, HALF, functools.partial(write_window, j))


def body(orbitals):
    nf = lax.axis_size("fft")
    nq = lax.axis_size("band") // 2
    rows = 256 // nq
    block = GRID * PLANES // nf
    tables = [jnp.asarray(table) for table in make_tables()]
    dma, vmem = pltpu.SemaphoreType.DMA, pltpu.VMEM
    local_out, window_out = pl.pallas_call(
        functools.partial(kernel, nf, nq),
        out_shape=(
            jax.ShapeDtypeStruct((2, PLANES, GRID * GRID), F32),
            jax.ShapeDtypeStruct((4, PLANES, GRID * GRID), F32),
        ),
        in_specs=[pl.BlockSpec(memory_space=pltpu.HBM)] * 6,
        out_specs=(pl.BlockSpec(memory_space=vmem),) * 2,
        scratch_shapes=[
            vmem((2, PLANES, GRID * GRID), F32),
            vmem((256, 256), BF16),
            vmem((256, 256), BF16),
            vmem((128, 256), BF16),
            vmem((128, 256), BF16),
            vmem((128, 256), BF16),
            vmem((PLANES * GRID, LANES), F32),
            vmem((4, PLANES * GRID, LANES), F32),
            vmem((GRID // nf, GRID, LANES), F32),
            vmem((4, PLANES, GRID * GRID), F32),
            vmem((4, PLANES * GRID, LANES), F32),
            vmem((4, nf, block, LANES), F32),
            vmem((4, PLANES * GRID, LANES), F32),
            vmem((4, nf, block, LANES), F32),
            vmem((4, 256, LANES), F32),
            vmem((2, 256, LANES), F32),
            vmem((2, 256, LANES), F32),
            vmem((2, nq, rows, LANES), F32),
            vmem((PLANES * GRID, LANES), F32),
            vmem((4, 256, LANES), F32),
            dma, dma((5,)), dma((2,)), dma((2,)), dma((2,)), dma((2,)), dma((2,)), dma((2,)),
            dma((4,)), dma((4,)), dma((4,)), dma((4,)),
            dma((2,)), dma((2,)), dma((2,)), dma((2,)),
            dma((2,)), dma((2,)), dma((2,)), dma((2,)),
        ],
        compiler_params=pltpu.CompilerParams(
            collective_id=0, has_side_effects=True, vmem_limit_bytes=56 * 1024 * 1024
        ),
        cost_estimate=pl.CostEstimate(
            flops=6 * 4 * 2 * 512 * 256 * 256, bytes_accessed=1 << 20, transcendentals=0
        ),
    )(orbitals, *tables)
    return local_out, window_out


def solution(mesh):
    return jax.shard_map(
        body,
        mesh=mesh,
        in_specs=(P("band", "fft", None),),
        out_specs=(P("band", "fft", None), P(None, "fft", None)),
        check_vma=False,
    )
```

```python
import functools
import math

import jax
import jax.numpy as jnp
import ml_dtypes
import numpy as np
from jax import lax
from jax.experimental import pallas as pl
from jax.experimental.pallas import tpu as pltpu
from jax.sharding import PartitionSpec as P

GRID = 64
LANES = 128
PLANES = 8
HALF = 32
SPACING = 0.367
MIXING = 0.25
MESH = pl.DeviceIdType.MESH
BF16 = jnp.bfloat16
F32 = jnp.float32


def split_table(table):
    high = table.astype(ml_dtypes.bfloat16)
    low = (table - high.astype(np.float64)).astype(ml_dtypes.bfloat16)
    return high, low


def make_tables():
    counter = np.arange(GRID)
    angles = (counter[:, None] * counter[None, :] % GRID) * (2.0 * np.pi / GRID)
    cosine, sine = np.cos(angles), np.sin(angles)
    depth = []
    for sign in (1.0, -1.0):
        table = np.block([[cosine, -sign * sine], [sign * sine, cosine]])
        high, low = split_table(table)
        row = np.concatenate([high, low], 1)
        depth.append(np.concatenate([row, row], 0))
    order = np.concatenate([np.arange(0, GRID, 2), np.arange(1, GRID, 2)])

    def stacked(rows, columns):
        table = np.concatenate(
            [cosine[np.ix_(rows, columns)], sine[np.ix_(rows, columns)]], 0
        )
        high, low = split_table(table)
        return np.concatenate([high, low, high, low], 1)

    return depth + [
        stacked(counter, order),
        stacked(counter, counter),
        stacked(order, counter),
    ]


def split_values(values):
    high = values.astype(BF16)
    low = (values - high.astype(F32)).astype(BF16)
    return high, low


def along_lanes(values, table):
    high, low = split_values(values)
    both = jnp.dot(jnp.concatenate([high, low], 1), table, preferred_element_type=F32)
    return both[:, :LANES] + both[:, LANES:]


def along_rows(first, second, table, sign):
    high, low = split_values(jnp.concatenate([first, second], 1))
    stack = jnp.concatenate([high, high, low, low], 0)
    both = jnp.dot(table, stack, preferred_element_type=F32)
    outs = []
    for index in range(2):
        columns = slice(index * LANES, (index + 1) * LANES)
        cos_part, sin_part = both[:GRID, columns], both[GRID:, columns]
        outs.append(cos_part + sign * pltpu.roll(sin_part, GRID, 1))
    return outs


def loop(first, last, step):
    def advance(index, carry):
        step(index)
        return carry

    lax.fori_loop(first, last, advance, 0, unroll=last - first)


def wait_for(ref, sem):
    pltpu.make_async_copy(ref, ref, sem).wait()


def kernel(
    nf, nq,
    orb_hbm, fz_hbm, iz_hbm, fy_hbm, fx_hbm, iy_hbm,
    local_ref, window_ref,
    orb, fz, iz, fy, fx, iy,
    obuf, dbuf, ktab, wbuf, fsend, frecv, bsend, brecv, part, pbuf, hbuf, rsbuf, acc, fin, lbuf,
    in_sem, table_sem, sc_s, sc_r, ag_s, ag_r, cx_s, cx_r, f_s, f_r, b_s, b_r,
    p_s, p_r, rs_s, rs_r, ga_s, ga_r, fx_s, fx_r, out_sem,
):
    band = lax.axis_index("band")
    me = lax.axis_index("fft")
    core = lax.rem(band, 2)
    chip = band // 2
    other = band + 1 - 2 * core
    second_root = nq
    root_chip = second_root // 2
    rows = 256 // nq
    columns = 2
    levels = nq // columns
    level, column = chip // columns, lax.rem(chip, columns)
    width = GRID * GRID // levels

    barrier = pltpu.get_barrier_semaphore()

    def signal(b, f):
        pl.semaphore_signal(barrier, inc=1, device_id=(b, f), device_id_type=MESH)

    @pl.when(jnp.logical_and(core == 0, chip != 0))
    def _():
        signal(0, me)

    @pl.when(jnp.logical_and(core == 1, chip != root_chip))
    def _():
        signal(second_root, me)

    loop(1, nf, lambda step: signal(band, lax.rem(me + step, nf)))
    signal(other, me)

    loads = [pltpu.make_async_copy(orb_hbm, orb, in_sem)]
    loads += [
        pltpu.make_async_copy(source, target, table_sem.at[index])
        for index, (source, target) in enumerate(
            ((fz_hbm, fz), (iz_hbm, iz), (fy_hbm, fy), (fx_hbm, fx), (iy_hbm, iy))
        )
    ]
    for load in loads:
        load.start()
    loads[0].wait()

    extra = jnp.where(jnp.logical_or(band == 0, band == second_root), nq - 1, 0)
    pl.semaphore_wait(barrier, nf - 1 + 1 + extra)

    def span(place):
        return pl.ds(pl.multiple_of(place * width, width), width)

    def scatter(window, root, p):
        piece = span(p // columns)
        pltpu.make_async_remote_copy(
            orb.at[window, :, piece], wbuf.at[2 * root + window, :, piece],
            sc_s.at[window], sc_r.at[window],
            device_id=(2 * p + root, me), device_id_type=MESH,
        ).start()

    @pl.when(band == 0)
    def _():
        for window in range(2):
            pltpu.make_async_copy(
                orb.at[window, :, pl.ds(0, width)], wbuf.at[window, :, pl.ds(0, width)],
                sc_r.at[window],
            ).start()
            loop(1, nq, lambda p: scatter(window, 0, p))

    @pl.when(band == second_root)
    def _():
        for window in range(2):
            loop(0, nq, lambda p: scatter(window, 1, p))

    lane = lax.broadcasted_iota(jnp.int32, (GRID, LANES), 1)
    low_lane = lane < GRID
    sign = jnp.where(low_lane, 1.0, -1.0).astype(F32)

    def fold(values):
        return jnp.where(2 * values < GRID, values, values - GRID)

    kz = fold(jnp.where(low_lane, lane, lane - GRID))
    kx = fold(lax.broadcasted_iota(jnp.int32, (GRID, LANES), 0))
    base = kx * kx + kz * kz
    factor = (2.0 * math.pi / (GRID * SPACING)) ** 2
    scale = -MIXING / GRID**3

    for row in range(GRID // nf):
        ky = fold(me * (GRID // nf) + row)
        squared = base + ky * ky
        clamped = jnp.maximum(squared, 1).astype(F32)
        ktab[row] = jnp.where(
            squared > 0, (4.0 * math.pi / factor * scale) / clamped, 0.0
        )

    tile_lane, half_lane = low_lane[:PLANES], low_lane[:HALF]

    def tile(t):
        return pl.ds(pl.multiple_of(t * LANES, LANES), LANES)

    def pack_orbitals(t):
        first, second = orb[0, :, tile(t)], orb[1, :, tile(t)]
        obuf[pl.ds(t, PLANES, stride=GRID), :] = jnp.where(
            tile_lane, first, pltpu.roll(second, GRID, 1)
        )
        obuf[pl.ds(t + HALF, PLANES, stride=GRID), :] = jnp.where(
            tile_lane, pltpu.roll(first, GRID, 1), second
        )

    loop(0, HALF, pack_orbitals)
    for load in loads[1:]:
        load.wait()

    def gather(window):
        mine = wbuf.at[2 * core + window, :, span(level)]
        wait_for(wbuf.at[window, :, pl.ds(0, width)], sc_r.at[window])

        def send(step):
            p = lax.rem(level + step, levels) * columns + column
            pltpu.make_async_remote_copy(
                mine, mine, ag_s.at[window], ag_r.at[window],
                device_id=(2 * p + core, me), device_id_type=MESH,
            ).start()

        loop(1, levels, send)

    def cross(window):
        wait_for(wbuf.at[window, :, pl.ds(0, (levels - 1) * width)], ag_r.at[window])
        whole = wbuf.at[2 * core + window]
        pltpu.make_async_remote_copy(
            whole, whole, cx_s.at[window], cx_r.at[window],
            device_id=(other, me), device_id_type=MESH,
        ).start()

    block = GRID * PLANES // nf

    def exchange(source, target, send_sem, recv_sem, k):
        own = pl.ds(pl.multiple_of(me * block, block), block)
        pltpu.make_async_copy(source.at[k, own, :], target.at[k, me], recv_sem.at[k]).start()

        def send(step):
            p = lax.rem(me + step, nf)
            pltpu.make_async_remote_copy(
                source.at[k, pl.ds(pl.multiple_of(p * block, block), block), :],
                target.at[k, me], send_sem.at[k], recv_sem.at[k],
                device_id=(band, p), device_id_type=MESH,
            ).start()

        loop(1, nf, send)

    def forward(k):
        j = lax.rem(2 * core + k, 4)

        def widen(t):
            values = wbuf[j, :, tile(t)]
            turned = pltpu.roll(values, GRID, 1)
            dbuf[k, pl.ds(t, PLANES, stride=GRID), :] = jnp.where(tile_lane, values, turned)
            dbuf[k, pl.ds(t + HALF, PLANES, stride=GRID), :] = jnp.where(
                tile_lane, turned, values
            )

        loop(0, HALF, widen)

        def step(i):
            both = pl.ds(pl.multiple_of(i * 2 * GRID, 2 * GRID), 2 * GRID)
            field = along_lanes(obuf[both, :] * dbuf[k, both, :], fz[...])
            outs = along_rows(field[:GRID], field[GRID:], fy[...], sign)
            for inner in range(2):
                fsend[k, pl.ds(2 * i + inner, GRID, stride=PLANES), :] = outs[inner]

        loop(0, PLANES // 2, step)
        exchange(fsend, frecv, f_s, f_r, k)

    def middle(k):
        wait_for(frecv.at[k], f_r.at[k])

        def step(i):
            pair = []
            for inner in range(2):
                start = pl.multiple_of((2 * i + inner) * PLANES, PLANES)
                pair.append(frecv[k, :, pl.ds(start, PLANES), :].reshape(GRID, LANES))
            outs = along_rows(pair[0], pair[1], fx[...], sign)
            outs = [outs[inner] * ktab[2 * i + inner] for inner in range(2)]
            outs = along_rows(outs[0], outs[1], fx[...], -sign)
            for inner in range(2):
                bsend[k, pl.ds(2 * i + inner, GRID, stride=PLANES), :] = outs[inner]

        loop(0, GRID // nf // 2, step)
        exchange(bsend, brecv, b_s, b_r, k)

    def backward(k):
        wait_for(brecv.at[k], b_r.at[k])

        def step(i):
            pair = []
            for inner in range(2):
                start = pl.multiple_of((2 * i + inner) * PLANES, PLANES)
                pair.append(brecv[k, :, pl.ds(start, PLANES), :].reshape(GRID, LANES))
            outs = along_rows(pair[0], pair[1], iy[...], -sign)
            potential = along_lanes(jnp.concatenate(outs, 0), iz[...])
            both = pl.ds(pl.multiple_of(i * 2 * GRID, 2 * GRID), 2 * GRID)
            term = dbuf[k, both, :] * potential
            if k == 0:
                acc[both, :] = term
            else:
                acc[both, :] += term
            product = obuf[both, :] * potential
            total = product + pltpu.roll(product, GRID, 1)
            for inner in range(2):
                start = inner * GRID
                part[k, pl.ds(2 * i + inner, HALF, stride=PLANES), :] = jnp.where(
                    half_lane, total[start:start + HALF], total[start + HALF:start + GRID]
                )

        loop(0, PLANES // 2, step)

    own_piece = pl.ds(pl.multiple_of(chip * rows, rows), rows)

    def to_partner(source, target, send_sem, recv_sem):
        pltpu.make_async_remote_copy(
            source, target, send_sem, recv_sem, device_id=(other, me), device_id_type=MESH
        ).start()

    def scatter_sum(k):
        wait_for(pbuf.at[k], p_r.at[k])
        hbuf[k] = part[k + 2] + pbuf[k]
        rsbuf[k, chip] = hbuf[k, own_piece, :]

        def send(step):
            p = lax.rem(chip + step, nq)
            pltpu.make_async_remote_copy(
                hbuf.at[k, pl.ds(pl.multiple_of(p * rows, rows), rows), :], rsbuf.at[k, chip],
                rs_s.at[k], rs_r.at[k], device_id=(2 * p + core, me), device_id_type=MESH,
            ).start()

        loop(1, nq, send)

    theirs = 2 - 2 * core
    share = rows * LANES // PLANES

    def gather_sum(k):
        wait_for(rsbuf.at[k, pl.ds(0, nq - 1)], rs_r.at[k])
        total = rsbuf[k, 0]
        for slot in range(1, nq):
            total = total + rsbuf[k, slot]
        for index in range(rows // PLANES):
            start = pl.multiple_of(chip * share + index * LANES, LANES)
            fin[theirs + k, :, pl.ds(start, LANES)] = total[index * PLANES:(index + 1) * PLANES]
        mine = fin.at[theirs + k, :, pl.ds(pl.multiple_of(chip * share, share), share)]

        def send(step):
            p = lax.rem(chip + step, nq)
            pltpu.make_async_remote_copy(
                mine, mine,
                ga_s.at[k], ga_r.at[k], device_id=(2 * p + core, me), device_id_type=MESH,
            ).start()

        loop(1, nq, send)

    def store(source, target, index):
        pltpu.make_async_copy(source, target, out_sem.at[index]).start()

    def share_sum(k):
        wait_for(fin.at[k, :, pl.ds(0, (nq - 1) * share)], ga_r.at[k])
        to_partner(fin.at[theirs + k], fin.at[theirs + k], fx_s.at[k], fx_r.at[k])
        store(fin.at[theirs + k], window_ref.at[theirs + k], 1 + k)

    gather(0)
    gather(1)
    for window in range(2):
        cross(window)
        forward(window)
    for window in range(2):
        wait_for(wbuf.at[window], cx_r.at[window])
        forward(window + 2)
    for k in range(4):
        middle(k)
    for k in range(2):
        backward(k)
        to_partner(part.at[k], pbuf.at[k], p_s.at[k], p_r.at[k])
    for k in range(2):
        backward(k + 2)
        scatter_sum(k)

    def unpack(t):
        even = acc[pl.ds(t, PLANES, stride=GRID), :]
        odd = acc[pl.ds(t + HALF, PLANES, stride=GRID), :]
        lbuf[0, :, tile(t)] = jnp.where(tile_lane, even, pltpu.roll(odd, GRID, 1))
        lbuf[1, :, tile(t)] = jnp.where(tile_lane, pltpu.roll(even, GRID, 1), odd)

    loop(0, HALF, unpack)
    store(lbuf, local_ref, 0)
    for k in range(2):
        gather_sum(k)
    for k in range(2):
        share_sum(k)
    for k in range(2):
        wait_for(fin.at[k], fx_r.at[k])
        store(fin.at[2 * core + k], window_ref.at[2 * core + k], 3 + k)

    @pl.when(band == 0)
    def _():
        for window in range(2):
            sent = (nq - 1) * PLANES * width // LANES
            wait_for(fsend.at[0, pl.ds(0, sent), :], sc_s.at[window])

    @pl.when(band == second_root)
    def _():
        for window in range(2):
            sent = nq * PLANES * width // LANES
            wait_for(fsend.at[0, pl.ds(0, sent), :], sc_s.at[window])

    for window in range(2):
        wait_for(wbuf.at[window, :, pl.ds(0, (levels - 1) * width)], ag_s.at[window])
        wait_for(wbuf.at[window], cx_s.at[window])
    for k in range(4):
        wait_for(frecv.at[k, pl.ds(0, nf - 1)], f_s.at[k])
        wait_for(brecv.at[k, pl.ds(0, nf - 1)], b_s.at[k])
    for k in range(2):
        wait_for(pbuf.at[k], p_s.at[k])
        wait_for(rsbuf.at[k, pl.ds(0, nq - 1)], rs_s.at[k])
        wait_for(fin.at[k, :, pl.ds(0, (nq - 1) * share)], ga_s.at[k])
        wait_for(fin.at[k], fx_s.at[k])
    wait_for(lbuf, out_sem.at[0])
    for index in range(4):
        wait_for(fin.at[index], out_sem.at[1 + index])


def body(orbitals):
    nf = lax.axis_size("fft")
    nq = lax.axis_size("band") // 2
    rows = 256 // nq
    block = GRID * PLANES // nf
    tables = [jnp.asarray(table) for table in make_tables()]
    dma, vmem = pltpu.SemaphoreType.DMA, pltpu.VMEM
    local_out, window_out = pl.pallas_call(
        functools.partial(kernel, nf, nq),
        out_shape=(
            jax.ShapeDtypeStruct((2, PLANES, GRID * GRID), F32),
            jax.ShapeDtypeStruct((4, PLANES, GRID * GRID), F32),
        ),
        in_specs=[pl.BlockSpec(memory_space=pltpu.HBM)] * 6,
        out_specs=(pl.BlockSpec(memory_space=pltpu.HBM),) * 2,
        scratch_shapes=[
            vmem((2, PLANES, GRID * GRID), F32),
            vmem((256, 256), BF16),
            vmem((256, 256), BF16),
            vmem((128, 256), BF16),
            vmem((128, 256), BF16),
            vmem((128, 256), BF16),
            vmem((PLANES * GRID, LANES), F32),
            vmem((4, PLANES * GRID, LANES), F32),
            vmem((GRID // nf, GRID, LANES), F32),
            vmem((4, PLANES, GRID * GRID), F32),
            vmem((4, PLANES * GRID, LANES), F32),
            vmem((4, nf, block, LANES), F32),
            vmem((4, PLANES * GRID, LANES), F32),
            vmem((4, nf, block, LANES), F32),
            vmem((4, 256, LANES), F32),
            vmem((2, 256, LANES), F32),
            vmem((2, 256, LANES), F32),
            vmem((2, nq, rows, LANES), F32),
            vmem((PLANES * GRID, LANES), F32),
            vmem((4, PLANES, GRID * GRID), F32),
            vmem((2, PLANES, GRID * GRID), F32),
            dma, dma((5,)), dma((2,)), dma((2,)), dma((2,)), dma((2,)), dma((2,)), dma((2,)),
            dma((4,)), dma((4,)), dma((4,)), dma((4,)),
            dma((2,)), dma((2,)), dma((2,)), dma((2,)),
            dma((2,)), dma((2,)), dma((2,)), dma((2,)), dma((5,)),
        ],
        compiler_params=pltpu.CompilerParams(
            collective_id=0, has_side_effects=True, vmem_limit_bytes=56 * 1024 * 1024
        ),
        cost_estimate=pl.CostEstimate(
            flops=6 * 4 * 2 * 512 * 256 * 256, bytes_accessed=1 << 20, transcendentals=0
        ),
    )(orbitals, *tables)
    return local_out, window_out


def solution(mesh):
    return jax.shard_map(
        body,
        mesh=mesh,
        in_specs=(P("band", "fft", None),),
        out_specs=(P("band", "fft", None), P(None, "fft", None)),
        check_vma=False,
    )
```

```python
import functools
import math

import jax
import jax.numpy as jnp
import ml_dtypes
import numpy as np
from jax import lax
from jax.experimental import pallas as pl
from jax.experimental.pallas import tpu as pltpu
from jax.sharding import PartitionSpec as P

GRID = 64
LANES = 128
PLANES = 8
HALF = 32
SPACING = 0.367
MIXING = 0.25
MESH = pl.DeviceIdType.MESH
BF16 = jnp.bfloat16
F32 = jnp.float32


def split_table(table):
    high = table.astype(ml_dtypes.bfloat16)
    low = (table - high.astype(np.float64)).astype(ml_dtypes.bfloat16)
    return high, low


def make_tables():
    counter = np.arange(GRID)
    angles = (counter[:, None] * counter[None, :] % GRID) * (2.0 * np.pi / GRID)
    cosine, sine = np.cos(angles), np.sin(angles)
    depth = []
    for sign in (1.0, -1.0):
        table = np.block([[cosine, -sign * sine], [sign * sine, cosine]])
        high, low = split_table(table)
        row = np.concatenate([high, low], 1)
        depth.append(np.concatenate([row, row], 0))
    order = np.concatenate([np.arange(0, GRID, 2), np.arange(1, GRID, 2)])

    def stacked(rows, columns):
        table = np.concatenate(
            [cosine[np.ix_(rows, columns)], sine[np.ix_(rows, columns)]], 0
        )
        high, low = split_table(table)
        return np.concatenate([high, low, high, low], 1)

    return depth + [
        stacked(counter, order),
        stacked(counter, counter),
        stacked(order, counter),
    ]


def split_values(values):
    high = values.astype(BF16)
    low = (values - high.astype(F32)).astype(BF16)
    return high, low


def along_lanes(values, table):
    high, low = split_values(values)
    both = jnp.dot(jnp.concatenate([high, low], 1), table, preferred_element_type=F32)
    return both[:, :LANES] + both[:, LANES:]


def along_rows(first, second, table, sign):
    high, low = split_values(jnp.concatenate([first, second], 1))
    stack = jnp.concatenate([high, high, low, low], 0)
    both = jnp.dot(table, stack, preferred_element_type=F32)
    outs = []
    for index in range(2):
        columns = slice(index * LANES, (index + 1) * LANES)
        cos_part, sin_part = both[:GRID, columns], both[GRID:, columns]
        outs.append(cos_part + sign * pltpu.roll(sin_part, GRID, 1))
    return outs


def loop(first, last, step):
    def advance(index, carry):
        step(index)
        return carry

    lax.fori_loop(first, last, advance, 0, unroll=last - first)


def far_first(count, step):
    half = count // 2
    loop(0, count - 1, lambda i: step(half + (1 - 2 * lax.rem(i, 2)) * ((i + 1) // 2)))


def wait_for(ref, sem):
    pltpu.make_async_copy(ref, ref, sem).wait()


def kernel(
    nf, nq,
    orb_hbm, fz_hbm, iz_hbm, fy_hbm, fx_hbm, iy_hbm,
    local_ref, window_ref,
    orb, fz, iz, fy, fx, iy,
    obuf, dbuf, ktab, wbuf, fsend, frecv, bsend, brecv, part, pbuf, hbuf, rsbuf, acc, fin, lbuf,
    in_sem, table_sem, sc_s, sc_r, ag_s, ag_r, cx_s, cx_r, f_s, f_r, b_s, b_r,
    p_s, p_r, rs_s, rs_r, ga_s, ga_r, fx_s, fx_r, out_sem,
):
    band = lax.axis_index("band")
    me = lax.axis_index("fft")
    core = lax.rem(band, 2)
    chip = band // 2
    other = band + 1 - 2 * core
    second_root = nq
    root_chip = second_root // 2
    rows = 256 // nq
    columns = 2
    levels = nq // columns
    level, column = chip // columns, lax.rem(chip, columns)
    width = GRID * GRID // levels

    barrier = pltpu.get_barrier_semaphore()

    def signal(b, f):
        pl.semaphore_signal(barrier, inc=1, device_id=(b, f), device_id_type=MESH)

    @pl.when(jnp.logical_and(core == 0, chip != 0))
    def _():
        signal(0, me)

    @pl.when(jnp.logical_and(core == 1, chip != root_chip))
    def _():
        signal(second_root, me)

    loop(1, nf, lambda step: signal(band, lax.rem(me + step, nf)))
    signal(other, me)

    loads = [pltpu.make_async_copy(orb_hbm, orb, in_sem)]
    loads += [
        pltpu.make_async_copy(source, target, table_sem.at[index])
        for index, (source, target) in enumerate(
            ((fz_hbm, fz), (iz_hbm, iz), (fy_hbm, fy), (fx_hbm, fx), (iy_hbm, iy))
        )
    ]
    for load in loads:
        load.start()
    loads[0].wait()

    extra = jnp.where(jnp.logical_or(band == 0, band == second_root), nq - 1, 0)
    pl.semaphore_wait(barrier, nf - 1 + 1 + extra)

    def span(place):
        return pl.ds(pl.multiple_of(place * width, width), width)

    def scatter(window, root, p):
        piece = span(p // columns)
        pltpu.make_async_remote_copy(
            orb.at[window, :, piece], wbuf.at[2 * root + window, :, piece],
            sc_s.at[window], sc_r.at[window],
            device_id=(2 * p + root, me), device_id_type=MESH,
        ).start()

    @pl.when(band == 0)
    def _():
        for window in range(2):
            pltpu.make_async_copy(
                orb.at[window, :, pl.ds(0, width)], wbuf.at[window, :, pl.ds(0, width)],
                sc_r.at[window],
            ).start()
            far_first(nq, lambda step: scatter(window, 0, step))

    @pl.when(band == second_root)
    def _():
        for window in range(2):
            far_first(nq, lambda step: scatter(window, 1, lax.rem(chip + step, nq)))
            scatter(window, 1, chip)

    lane = lax.broadcasted_iota(jnp.int32, (GRID, LANES), 1)
    low_lane = lane < GRID
    sign = jnp.where(low_lane, 1.0, -1.0).astype(F32)

    def fold(values):
        return jnp.where(2 * values < GRID, values, values - GRID)

    kz = fold(jnp.where(low_lane, lane, lane - GRID))
    kx = fold(lax.broadcasted_iota(jnp.int32, (GRID, LANES), 0))
    base = kx * kx + kz * kz
    factor = (2.0 * math.pi / (GRID * SPACING)) ** 2
    scale = -MIXING / GRID**3

    for row in range(GRID // nf):
        ky = fold(me * (GRID // nf) + row)
        squared = base + ky * ky
        clamped = jnp.maximum(squared, 1).astype(F32)
        ktab[row] = jnp.where(
            squared > 0, (4.0 * math.pi / factor * scale) / clamped, 0.0
        )

    tile_lane, half_lane = low_lane[:PLANES], low_lane[:HALF]

    def tile(t):
        return pl.ds(pl.multiple_of(t * LANES, LANES), LANES)

    def pack_orbitals(t):
        first, second = orb[0, :, tile(t)], orb[1, :, tile(t)]
        obuf[pl.ds(t, PLANES, stride=GRID), :] = jnp.where(
            tile_lane, first, pltpu.roll(second, GRID, 1)
        )
        obuf[pl.ds(t + HALF, PLANES, stride=GRID), :] = jnp.where(
            tile_lane, pltpu.roll(first, GRID, 1), second
        )

    loop(0, HALF, pack_orbitals)
    for load in loads[1:]:
        load.wait()

    def gather(window):
        mine = wbuf.at[2 * core + window, :, span(level)]
        wait_for(wbuf.at[window, :, pl.ds(0, width)], sc_r.at[window])

        def send(step):
            p = lax.rem(level + step, levels) * columns + column
            pltpu.make_async_remote_copy(
                mine, mine, ag_s.at[window], ag_r.at[window],
                device_id=(2 * p + core, me), device_id_type=MESH,
            ).start()

        far_first(levels, send)

    def cross(window):
        wait_for(wbuf.at[window, :, pl.ds(0, (levels - 1) * width)], ag_r.at[window])
        whole = wbuf.at[2 * core + window]
        pltpu.make_async_remote_copy(
            whole, whole, cx_s.at[window], cx_r.at[window],
            device_id=(other, me), device_id_type=MESH,
        ).start()

    block = GRID * PLANES // nf

    def exchange(source, target, send_sem, recv_sem, k):
        own = pl.ds(pl.multiple_of(me * block, block), block)
        pltpu.make_async_copy(source.at[k, own, :], target.at[k, me], recv_sem.at[k]).start()

        def send(step):
            p = lax.rem(me + step, nf)
            pltpu.make_async_remote_copy(
                source.at[k, pl.ds(pl.multiple_of(p * block, block), block), :],
                target.at[k, me], send_sem.at[k], recv_sem.at[k],
                device_id=(band, p), device_id_type=MESH,
            ).start()

        loop(1, nf, send)

    def forward(k):
        j = lax.rem(2 * core + k, 4)

        def widen(t):
            values = wbuf[j, :, tile(t)]
            turned = pltpu.roll(values, GRID, 1)
            dbuf[k, pl.ds(t, PLANES, stride=GRID), :] = jnp.where(tile_lane, values, turned)
            dbuf[k, pl.ds(t + HALF, PLANES, stride=GRID), :] = jnp.where(
                tile_lane, turned, values
            )

        loop(0, HALF, widen)

        def step(i):
            both = pl.ds(pl.multiple_of(i * 2 * GRID, 2 * GRID), 2 * GRID)
            field = along_lanes(obuf[both, :] * dbuf[k, both, :], fz[...])
            outs = along_rows(field[:GRID], field[GRID:], fy[...], sign)
            for inner in range(2):
                fsend[k, pl.ds(2 * i + inner, GRID, stride=PLANES), :] = outs[inner]

        loop(0, PLANES // 2, step)
        exchange(fsend, frecv, f_s, f_r, k)

    def middle(k):
        wait_for(frecv.at[k], f_r.at[k])

        def step(i):
            pair = []
            for inner in range(2):
                start = pl.multiple_of((2 * i + inner) * PLANES, PLANES)
                pair.append(frecv[k, :, pl.ds(start, PLANES), :].reshape(GRID, LANES))
            outs = along_rows(pair[0], pair[1], fx[...], sign)
            outs = [outs[inner] * ktab[2 * i + inner] for inner in range(2)]
            outs = along_rows(outs[0], outs[1], fx[...], -sign)
            for inner in range(2):
                bsend[k, pl.ds(2 * i + inner, GRID, stride=PLANES), :] = outs[inner]

        loop(0, GRID // nf // 2, step)
        exchange(bsend, brecv, b_s, b_r, k)

    def backward(k):
        wait_for(brecv.at[k], b_r.at[k])

        def step(i):
            pair = []
            for inner in range(2):
                start = pl.multiple_of((2 * i + inner) * PLANES, PLANES)
                pair.append(brecv[k, :, pl.ds(start, PLANES), :].reshape(GRID, LANES))
            outs = along_rows(pair[0], pair[1], iy[...], -sign)
            potential = along_lanes(jnp.concatenate(outs, 0), iz[...])
            both = pl.ds(pl.multiple_of(i * 2 * GRID, 2 * GRID), 2 * GRID)
            term = dbuf[k, both, :] * potential
            if k == 0:
                acc[both, :] = term
            else:
                acc[both, :] += term
            product = obuf[both, :] * potential
            total = product + pltpu.roll(product, GRID, 1)
            for inner in range(2):
                start = inner * GRID
                part[k, pl.ds(2 * i + inner, HALF, stride=PLANES), :] = jnp.where(
                    half_lane, total[start:start + HALF], total[start + HALF:start + GRID]
                )

        loop(0, PLANES // 2, step)

    own_piece = pl.ds(pl.multiple_of(chip * rows, rows), rows)

    def to_partner(source, target, send_sem, recv_sem):
        pltpu.make_async_remote_copy(
            source, target, send_sem, recv_sem, device_id=(other, me), device_id_type=MESH
        ).start()

    def scatter_sum(k):
        wait_for(pbuf.at[k], p_r.at[k])
        hbuf[k] = part[k + 2] + pbuf[k]
        rsbuf[k, chip] = hbuf[k, own_piece, :]

        def send(step):
            p = lax.rem(chip + step, nq)
            pltpu.make_async_remote_copy(
                hbuf.at[k, pl.ds(pl.multiple_of(p * rows, rows), rows), :], rsbuf.at[k, chip],
                rs_s.at[k], rs_r.at[k], device_id=(2 * p + core, me), device_id_type=MESH,
            ).start()

        far_first(nq, send)

    theirs = 2 - 2 * core
    share = rows * LANES // PLANES

    def gather_sum(k):
        wait_for(rsbuf.at[k, pl.ds(0, nq - 1)], rs_r.at[k])
        total = rsbuf[k, 0]
        for slot in range(1, nq):
            total = total + rsbuf[k, slot]
        for index in range(rows // PLANES):
            start = pl.multiple_of(chip * share + index * LANES, LANES)
            fin[theirs + k, :, pl.ds(start, LANES)] = total[index * PLANES:(index + 1) * PLANES]
        mine = fin.at[theirs + k, :, pl.ds(pl.multiple_of(chip * share, share), share)]

        def send(step):
            p = lax.rem(chip + step, nq)
            pltpu.make_async_remote_copy(
                mine, mine,
                ga_s.at[k], ga_r.at[k], device_id=(2 * p + core, me), device_id_type=MESH,
            ).start()

        far_first(nq, send)

    def store(source, target, index):
        pltpu.make_async_copy(source, target, out_sem.at[index]).start()

    def share_sum(k):
        wait_for(fin.at[k, :, pl.ds(0, (nq - 1) * share)], ga_r.at[k])
        to_partner(fin.at[theirs + k], fin.at[theirs + k], fx_s.at[k], fx_r.at[k])
        store(fin.at[theirs + k], window_ref.at[theirs + k], 1 + k)

    gather(0)
    gather(1)
    for window in range(2):
        cross(window)
        forward(window)
    for window in range(2):
        wait_for(wbuf.at[window], cx_r.at[window])
        forward(window + 2)
    for k in range(4):
        middle(k)
    for k in range(2):
        backward(k)
        to_partner(part.at[k], pbuf.at[k], p_s.at[k], p_r.at[k])
    for k in range(2):
        backward(k + 2)
        scatter_sum(k)

    def unpack(t):
        even = acc[pl.ds(t, PLANES, stride=GRID), :]
        odd = acc[pl.ds(t + HALF, PLANES, stride=GRID), :]
        lbuf[0, :, tile(t)] = jnp.where(tile_lane, even, pltpu.roll(odd, GRID, 1))
        lbuf[1, :, tile(t)] = jnp.where(tile_lane, pltpu.roll(even, GRID, 1), odd)

    loop(0, HALF, unpack)
    store(lbuf, local_ref, 0)
    for k in range(2):
        gather_sum(k)
    for k in range(2):
        share_sum(k)
    for k in range(2):
        wait_for(fin.at[k], fx_r.at[k])
        store(fin.at[2 * core + k], window_ref.at[2 * core + k], 3 + k)

    @pl.when(band == 0)
    def _():
        for window in range(2):
            sent = (nq - 1) * PLANES * width // LANES
            wait_for(fsend.at[0, pl.ds(0, sent), :], sc_s.at[window])

    @pl.when(band == second_root)
    def _():
        for window in range(2):
            sent = nq * PLANES * width // LANES
            wait_for(fsend.at[0, pl.ds(0, sent), :], sc_s.at[window])

    for window in range(2):
        wait_for(wbuf.at[window, :, pl.ds(0, (levels - 1) * width)], ag_s.at[window])
        wait_for(wbuf.at[window], cx_s.at[window])
    for k in range(4):
        wait_for(frecv.at[k, pl.ds(0, nf - 1)], f_s.at[k])
        wait_for(brecv.at[k, pl.ds(0, nf - 1)], b_s.at[k])
    for k in range(2):
        wait_for(pbuf.at[k], p_s.at[k])
        wait_for(rsbuf.at[k, pl.ds(0, nq - 1)], rs_s.at[k])
        wait_for(fin.at[k, :, pl.ds(0, (nq - 1) * share)], ga_s.at[k])
        wait_for(fin.at[k], fx_s.at[k])
    wait_for(lbuf, out_sem.at[0])
    for index in range(4):
        wait_for(fin.at[index], out_sem.at[1 + index])


def body(orbitals):
    nf = lax.axis_size("fft")
    nq = lax.axis_size("band") // 2
    rows = 256 // nq
    block = GRID * PLANES // nf
    tables = [jnp.asarray(table) for table in make_tables()]
    dma, vmem = pltpu.SemaphoreType.DMA, pltpu.VMEM
    local_out, window_out = pl.pallas_call(
        functools.partial(kernel, nf, nq),
        out_shape=(
            jax.ShapeDtypeStruct((2, PLANES, GRID * GRID), F32),
            jax.ShapeDtypeStruct((4, PLANES, GRID * GRID), F32),
        ),
        in_specs=[pl.BlockSpec(memory_space=pltpu.HBM)] * 6,
        out_specs=(pl.BlockSpec(memory_space=pltpu.HBM),) * 2,
        scratch_shapes=[
            vmem((2, PLANES, GRID * GRID), F32),
            vmem((256, 256), BF16),
            vmem((256, 256), BF16),
            vmem((128, 256), BF16),
            vmem((128, 256), BF16),
            vmem((128, 256), BF16),
            vmem((PLANES * GRID, LANES), F32),
            vmem((4, PLANES * GRID, LANES), F32),
            vmem((GRID // nf, GRID, LANES), F32),
            vmem((4, PLANES, GRID * GRID), F32),
            vmem((4, PLANES * GRID, LANES), F32),
            vmem((4, nf, block, LANES), F32),
            vmem((4, PLANES * GRID, LANES), F32),
            vmem((4, nf, block, LANES), F32),
            vmem((4, 256, LANES), F32),
            vmem((2, 256, LANES), F32),
            vmem((2, 256, LANES), F32),
            vmem((2, nq, rows, LANES), F32),
            vmem((PLANES * GRID, LANES), F32),
            vmem((4, PLANES, GRID * GRID), F32),
            vmem((2, PLANES, GRID * GRID), F32),
            dma, dma((5,)), dma((2,)), dma((2,)), dma((2,)), dma((2,)), dma((2,)), dma((2,)),
            dma((4,)), dma((4,)), dma((4,)), dma((4,)),
            dma((2,)), dma((2,)), dma((2,)), dma((2,)),
            dma((2,)), dma((2,)), dma((2,)), dma((2,)), dma((5,)),
        ],
        compiler_params=pltpu.CompilerParams(
            collective_id=0, has_side_effects=True, vmem_limit_bytes=40 * 1024 * 1024
        ),
        cost_estimate=pl.CostEstimate(
            flops=6 * 4 * 2 * 512 * 256 * 256, bytes_accessed=1 << 20, transcendentals=0
        ),
    )(*[pltpu.with_memory_space_constraint(a, pltpu.HBM) for a in (orbitals, *tables)])
    return local_out, window_out


def solution(mesh):
    return jax.shard_map(
        body,
        mesh=mesh,
        in_specs=(P("band", "fft", None),),
        out_specs=(P("band", "fft", None), P(None, "fft", None)),
        check_vma=False,
    )
```

```python
import functools
import math

import jax
import jax.numpy as jnp
import ml_dtypes
import numpy as np
from jax import lax
from jax.experimental import pallas as pl
from jax.experimental.pallas import tpu as pltpu
from jax.sharding import PartitionSpec as P

GRID = 64
LANES = 128
PLANES = 8
HALF = 32
SPACING = 0.367
MIXING = 0.25
MESH = pl.DeviceIdType.MESH
BF16 = jnp.bfloat16
F32 = jnp.float32


def split_table(table):
    high = table.astype(ml_dtypes.bfloat16)
    low = (table - high.astype(np.float64)).astype(ml_dtypes.bfloat16)
    return high, low


def make_tables():
    counter = np.arange(GRID)
    angles = (counter[:, None] * counter[None, :] % GRID) * (2.0 * np.pi / GRID)
    cosine, sine = np.cos(angles), np.sin(angles)
    depth = []
    for sign in (1.0, -1.0):
        table = np.block([[cosine, -sign * sine], [sign * sine, cosine]])
        high, low = split_table(table)
        row = np.concatenate([high, low], 1)
        depth.append(np.concatenate([row, row], 0))
    order = np.concatenate([np.arange(0, GRID, 2), np.arange(1, GRID, 2)])

    def stacked(rows, columns):
        table = np.concatenate(
            [cosine[np.ix_(rows, columns)], sine[np.ix_(rows, columns)]], 0
        )
        high, low = split_table(table)
        return np.concatenate([high, low, high, low], 1)

    return depth + [
        stacked(counter, order),
        stacked(counter, counter),
        stacked(order, counter),
    ]


def split_values(values):
    high = values.astype(BF16)
    low = (values - high.astype(F32)).astype(BF16)
    return high, low


def along_lanes(values, table):
    high, low = split_values(values)
    both = jnp.dot(jnp.concatenate([high, low], 1), table, preferred_element_type=F32)
    return both[:, :LANES] + both[:, LANES:]


def along_rows(first, second, table, sign):
    high, low = split_values(jnp.concatenate([first, second], 1))
    stack = jnp.concatenate([high, high, low, low], 0)
    both = jnp.dot(table, stack, preferred_element_type=F32)
    outs = []
    for index in range(2):
        columns = slice(index * LANES, (index + 1) * LANES)
        cos_part, sin_part = both[:GRID, columns], both[GRID:, columns]
        outs.append(cos_part + sign * pltpu.roll(sin_part, GRID, 1))
    return outs


def loop(first, last, step):
    def advance(index, carry):
        step(index)
        return carry

    lax.fori_loop(first, last, advance, 0, unroll=last - first)


def far_first(count, step):
    half = count // 2
    loop(0, count - 1, lambda i: step(half + (1 - 2 * lax.rem(i, 2)) * ((i + 1) // 2)))


def pairs_far_first(count, step):
    half = count // 2

    def both(i):
        k = i // 2
        step(half + (1 - 2 * lax.rem(k, 2)) * ((k + 1) // 2), 1 - lax.rem(i, 2))

    loop(0, 2 * count - 1, both)


def wait_for(ref, sem):
    pltpu.make_async_copy(ref, ref, sem).wait()


def kernel(
    nf, nq,
    orb_hbm, fz_hbm, iz_hbm, fy_hbm, fx_hbm, iy_hbm,
    local_ref, window_ref,
    orb, fz, iz, fy, fx, iy,
    obuf, dbuf, ktab, wbuf, fsend, frecv, bsend, brecv, part, pbuf, hbuf, rsbuf, acc, fin, lbuf,
    in_sem, table_sem, sc_s, sc_r, ag_s, ag_r, cx_s, cx_r, f_s, f_r, b_s, b_r,
    p_s, p_r, rs_s, rs_r, ga_s, ga_r, fx_s, fx_r, out_sem,
):
    band = lax.axis_index("band")
    me = lax.axis_index("fft")
    core = lax.rem(band, 2)
    chip = band // 2
    other = band + 1 - 2 * core
    second_root = nq
    root_chip = second_root // 2
    rows = 256 // nq
    columns = 2
    levels = nq // columns
    level, column = chip // columns, lax.rem(chip, columns)
    width = GRID * GRID // levels

    def chip_at(up, across):
        return lax.rem(level + up, levels) * columns + lax.rem(column + across, columns)


    barrier = pltpu.get_barrier_semaphore()

    def signal(b, f):
        pl.semaphore_signal(barrier, inc=1, device_id=(b, f), device_id_type=MESH)

    @pl.when(jnp.logical_and(core == 0, chip != 0))
    def _():
        signal(0, me)

    @pl.when(jnp.logical_and(core == 1, chip != root_chip))
    def _():
        signal(second_root, me)

    loop(1, nf, lambda step: signal(band, lax.rem(me + step, nf)))
    signal(other, me)

    loads = [pltpu.make_async_copy(orb_hbm, orb, in_sem)]
    loads += [
        pltpu.make_async_copy(source, target, table_sem.at[index])
        for index, (source, target) in enumerate(
            ((fz_hbm, fz), (iz_hbm, iz), (fy_hbm, fy), (fx_hbm, fx), (iy_hbm, iy))
        )
    ]
    for load in loads:
        load.start()
    loads[0].wait()

    extra = jnp.where(jnp.logical_or(band == 0, band == second_root), nq - 1, 0)
    pl.semaphore_wait(barrier, nf - 1 + 1 + extra)

    def span(place):
        return pl.ds(pl.multiple_of(place * width, width), width)

    def scatter(window, root, p):
        piece = span(p // columns)
        pltpu.make_async_remote_copy(
            orb.at[window, :, piece], wbuf.at[2 * root + window, :, piece],
            sc_s.at[window], sc_r.at[window],
            device_id=(2 * p + root, me), device_id_type=MESH,
        ).start()

    @pl.when(band == 0)
    def _():
        for window in range(2):
            pltpu.make_async_copy(
                orb.at[window, :, pl.ds(0, width)], wbuf.at[window, :, pl.ds(0, width)],
                sc_r.at[window],
            ).start()
            pairs_far_first(levels, lambda up, across: scatter(window, 0, chip_at(up, across)))

    @pl.when(band == second_root)
    def _():
        for window in range(2):
            pairs_far_first(levels, lambda up, across: scatter(window, 1, chip_at(up, across)))
            scatter(window, 1, chip)

    lane = lax.broadcasted_iota(jnp.int32, (GRID, LANES), 1)
    low_lane = lane < GRID
    sign = jnp.where(low_lane, 1.0, -1.0).astype(F32)

    def fold(values):
        return jnp.where(2 * values < GRID, values, values - GRID)

    kz = fold(jnp.where(low_lane, lane, lane - GRID))
    kx = fold(lax.broadcasted_iota(jnp.int32, (GRID, LANES), 0))
    base = kx * kx + kz * kz
    factor = (2.0 * math.pi / (GRID * SPACING)) ** 2
    scale = -MIXING / GRID**3

    for row in range(GRID // nf):
        ky = fold(me * (GRID // nf) + row)
        squared = base + ky * ky
        clamped = jnp.maximum(squared, 1).astype(F32)
        ktab[row] = jnp.where(
            squared > 0, (4.0 * math.pi / factor * scale) / clamped, 0.0
        )

    tile_lane, half_lane = low_lane[:PLANES], low_lane[:HALF]

    def tile(t):
        return pl.ds(pl.multiple_of(t * LANES, LANES), LANES)

    def pack_orbitals(t):
        first, second = orb[0, :, tile(t)], orb[1, :, tile(t)]
        obuf[pl.ds(t, PLANES, stride=GRID), :] = jnp.where(
            tile_lane, first, pltpu.roll(second, GRID, 1)
        )
        obuf[pl.ds(t + HALF, PLANES, stride=GRID), :] = jnp.where(
            tile_lane, pltpu.roll(first, GRID, 1), second
        )

    loop(0, HALF, pack_orbitals)
    for load in loads[1:]:
        load.wait()

    def gather(window):
        mine = wbuf.at[2 * core + window, :, span(level)]
        wait_for(wbuf.at[window, :, pl.ds(0, width)], sc_r.at[window])

        def send(step):
            p = lax.rem(level + step, levels) * columns + column
            pltpu.make_async_remote_copy(
                mine, mine, ag_s.at[window], ag_r.at[window],
                device_id=(2 * p + core, me), device_id_type=MESH,
            ).start()

        far_first(levels, send)

    def cross(window):
        wait_for(wbuf.at[window, :, pl.ds(0, (levels - 1) * width)], ag_r.at[window])
        whole = wbuf.at[2 * core + window]
        pltpu.make_async_remote_copy(
            whole, whole, cx_s.at[window], cx_r.at[window],
            device_id=(other, me), device_id_type=MESH,
        ).start()

    block = GRID * PLANES // nf

    def exchange(source, target, send_sem, recv_sem, k):
        own = pl.ds(pl.multiple_of(me * block, block), block)
        pltpu.make_async_copy(source.at[k, own, :], target.at[k, me], recv_sem.at[k]).start()

        def send(step):
            p = lax.rem(me + step, nf)
            pltpu.make_async_remote_copy(
                source.at[k, pl.ds(pl.multiple_of(p * block, block), block), :],
                target.at[k, me], send_sem.at[k], recv_sem.at[k],
                device_id=(band, p), device_id_type=MESH,
            ).start()

        loop(1, nf, send)

    def forward(k):
        j = lax.rem(2 * core + k, 4)

        def widen(t):
            values = wbuf[j, :, tile(t)]
            turned = pltpu.roll(values, GRID, 1)
            dbuf[k, pl.ds(t, PLANES, stride=GRID), :] = jnp.where(tile_lane, values, turned)
            dbuf[k, pl.ds(t + HALF, PLANES, stride=GRID), :] = jnp.where(
                tile_lane, turned, values
            )

        loop(0, HALF, widen)

        def step(i):
            both = pl.ds(pl.multiple_of(i * 2 * GRID, 2 * GRID), 2 * GRID)
            field = along_lanes(obuf[both, :] * dbuf[k, both, :], fz[...])
            outs = along_rows(field[:GRID], field[GRID:], fy[...], sign)
            for inner in range(2):
                fsend[k, pl.ds(2 * i + inner, GRID, stride=PLANES), :] = outs[inner]

        loop(0, PLANES // 2, step)
        exchange(fsend, frecv, f_s, f_r, k)

    def middle(k):
        wait_for(frecv.at[k], f_r.at[k])

        def step(i):
            pair = []
            for inner in range(2):
                start = pl.multiple_of((2 * i + inner) * PLANES, PLANES)
                pair.append(frecv[k, :, pl.ds(start, PLANES), :].reshape(GRID, LANES))
            outs = along_rows(pair[0], pair[1], fx[...], sign)
            outs = [outs[inner] * ktab[2 * i + inner] for inner in range(2)]
            outs = along_rows(outs[0], outs[1], fx[...], -sign)
            for inner in range(2):
                bsend[k, pl.ds(2 * i + inner, GRID, stride=PLANES), :] = outs[inner]

        loop(0, GRID // nf // 2, step)
        exchange(bsend, brecv, b_s, b_r, k)

    def backward(k):
        wait_for(brecv.at[k], b_r.at[k])

        def step(i):
            pair = []
            for inner in range(2):
                start = pl.multiple_of((2 * i + inner) * PLANES, PLANES)
                pair.append(brecv[k, :, pl.ds(start, PLANES), :].reshape(GRID, LANES))
            outs = along_rows(pair[0], pair[1], iy[...], -sign)
            potential = along_lanes(jnp.concatenate(outs, 0), iz[...])
            both = pl.ds(pl.multiple_of(i * 2 * GRID, 2 * GRID), 2 * GRID)
            term = dbuf[k, both, :] * potential
            if k == 0:
                acc[both, :] = term
            else:
                acc[both, :] += term
            product = obuf[both, :] * potential
            total = product + pltpu.roll(product, GRID, 1)
            for inner in range(2):
                start = inner * GRID
                part[k, pl.ds(2 * i + inner, HALF, stride=PLANES), :] = jnp.where(
                    half_lane, total[start:start + HALF], total[start + HALF:start + GRID]
                )

        loop(0, PLANES // 2, step)

    own_piece = pl.ds(pl.multiple_of(chip * rows, rows), rows)

    def to_partner(source, target, send_sem, recv_sem):
        pltpu.make_async_remote_copy(
            source, target, send_sem, recv_sem, device_id=(other, me), device_id_type=MESH
        ).start()

    def scatter_sum(k):
        wait_for(pbuf.at[k], p_r.at[k])
        hbuf[k] = part[k + 2] + pbuf[k]
        rsbuf[k, chip] = hbuf[k, own_piece, :]

        def send(up, across):
            p = chip_at(up, across)
            pltpu.make_async_remote_copy(
                hbuf.at[k, pl.ds(pl.multiple_of(p * rows, rows), rows), :], rsbuf.at[k, chip],
                rs_s.at[k], rs_r.at[k], device_id=(2 * p + core, me), device_id_type=MESH,
            ).start()

        pairs_far_first(levels, send)

    theirs = 2 - 2 * core
    share = rows * LANES // PLANES

    def gather_sum(k):
        wait_for(rsbuf.at[k, pl.ds(0, nq - 1)], rs_r.at[k])
        total = rsbuf[k, 0]
        for slot in range(1, nq):
            total = total + rsbuf[k, slot]
        for index in range(rows // PLANES):
            start = pl.multiple_of(chip * share + index * LANES, LANES)
            fin[theirs + k, :, pl.ds(start, LANES)] = total[index * PLANES:(index + 1) * PLANES]
        mine = fin.at[theirs + k, :, pl.ds(pl.multiple_of(chip * share, share), share)]

        def send(up, across):
            p = chip_at(up, across)
            pltpu.make_async_remote_copy(
                mine, mine,
                ga_s.at[k], ga_r.at[k], device_id=(2 * p + core, me), device_id_type=MESH,
            ).start()

        pairs_far_first(levels, send)

    def store(source, target, index):
        pltpu.make_async_copy(source, target, out_sem.at[index]).start()

    def share_sum(k):
        wait_for(fin.at[k, :, pl.ds(0, (nq - 1) * share)], ga_r.at[k])
        to_partner(fin.at[theirs + k], fin.at[theirs + k], fx_s.at[k], fx_r.at[k])
        store(fin.at[theirs + k], window_ref.at[theirs + k], 1 + k)

    gather(0)
    gather(1)
    for window in range(2):
        cross(window)
        forward(window)
    for window in range(2):
        wait_for(wbuf.at[window], cx_r.at[window])
        forward(window + 2)
    for k in range(4):
        middle(k)
    for k in range(2):
        backward(k)
        to_partner(part.at[k], pbuf.at[k], p_s.at[k], p_r.at[k])
    for k in range(2):
        backward(k + 2)
        scatter_sum(k)

    def unpack(t):
        even = acc[pl.ds(t, PLANES, stride=GRID), :]
        odd = acc[pl.ds(t + HALF, PLANES, stride=GRID), :]
        lbuf[0, :, tile(t)] = jnp.where(tile_lane, even, pltpu.roll(odd, GRID, 1))
        lbuf[1, :, tile(t)] = jnp.where(tile_lane, pltpu.roll(even, GRID, 1), odd)

    loop(0, HALF, unpack)
    store(lbuf, local_ref, 0)
    for k in range(2):
        gather_sum(k)
    for k in range(2):
        share_sum(k)
    for k in range(2):
        wait_for(fin.at[k], fx_r.at[k])
        store(fin.at[2 * core + k], window_ref.at[2 * core + k], 3 + k)

    @pl.when(band == 0)
    def _():
        for window in range(2):
            sent = (nq - 1) * PLANES * width // LANES
            wait_for(fsend.at[0, pl.ds(0, sent), :], sc_s.at[window])

    @pl.when(band == second_root)
    def _():
        for window in range(2):
            sent = nq * PLANES * width // LANES
            wait_for(fsend.at[0, pl.ds(0, sent), :], sc_s.at[window])

    for window in range(2):
        wait_for(wbuf.at[window, :, pl.ds(0, (levels - 1) * width)], ag_s.at[window])
        wait_for(wbuf.at[window], cx_s.at[window])
    for k in range(4):
        wait_for(frecv.at[k, pl.ds(0, nf - 1)], f_s.at[k])
        wait_for(brecv.at[k, pl.ds(0, nf - 1)], b_s.at[k])
    for k in range(2):
        wait_for(pbuf.at[k], p_s.at[k])
        wait_for(rsbuf.at[k, pl.ds(0, nq - 1)], rs_s.at[k])
        wait_for(fin.at[k, :, pl.ds(0, (nq - 1) * share)], ga_s.at[k])
        wait_for(fin.at[k], fx_s.at[k])
    wait_for(lbuf, out_sem.at[0])
    for index in range(4):
        wait_for(fin.at[index], out_sem.at[1 + index])


def body(orbitals):
    nf = lax.axis_size("fft")
    nq = lax.axis_size("band") // 2
    rows = 256 // nq
    block = GRID * PLANES // nf
    tables = [jnp.asarray(table) for table in make_tables()]
    dma, vmem = pltpu.SemaphoreType.DMA, pltpu.VMEM
    local_out, window_out = pl.pallas_call(
        functools.partial(kernel, nf, nq),
        out_shape=(
            jax.ShapeDtypeStruct((2, PLANES, GRID * GRID), F32),
            jax.ShapeDtypeStruct((4, PLANES, GRID * GRID), F32),
        ),
        in_specs=[pl.BlockSpec(memory_space=pltpu.HBM)] * 6,
        out_specs=(pl.BlockSpec(memory_space=pltpu.HBM),) * 2,
        scratch_shapes=[
            vmem((2, PLANES, GRID * GRID), F32),
            vmem((256, 256), BF16),
            vmem((256, 256), BF16),
            vmem((128, 256), BF16),
            vmem((128, 256), BF16),
            vmem((128, 256), BF16),
            vmem((PLANES * GRID, LANES), F32),
            vmem((4, PLANES * GRID, LANES), F32),
            vmem((GRID // nf, GRID, LANES), F32),
            vmem((4, PLANES, GRID * GRID), F32),
            vmem((4, PLANES * GRID, LANES), F32),
            vmem((4, nf, block, LANES), F32),
            vmem((4, PLANES * GRID, LANES), F32),
            vmem((4, nf, block, LANES), F32),
            vmem((4, 256, LANES), F32),
            vmem((2, 256, LANES), F32),
            vmem((2, 256, LANES), F32),
            vmem((2, nq, rows, LANES), F32),
            vmem((PLANES * GRID, LANES), F32),
            vmem((4, PLANES, GRID * GRID), F32),
            vmem((2, PLANES, GRID * GRID), F32),
            dma, dma((5,)), dma((2,)), dma((2,)), dma((2,)), dma((2,)), dma((2,)), dma((2,)),
            dma((4,)), dma((4,)), dma((4,)), dma((4,)),
            dma((2,)), dma((2,)), dma((2,)), dma((2,)),
            dma((2,)), dma((2,)), dma((2,)), dma((2,)), dma((5,)),
        ],
        compiler_params=pltpu.CompilerParams(
            collective_id=0, has_side_effects=True, vmem_limit_bytes=40 * 1024 * 1024
        ),
        cost_estimate=pl.CostEstimate(
            flops=6 * 4 * 2 * 512 * 256 * 256, bytes_accessed=1 << 20, transcendentals=0
        ),
    )(*[pltpu.with_memory_space_constraint(a, pltpu.HBM) for a in (orbitals, *tables)])
    return local_out, window_out


def solution(mesh):
    return jax.shard_map(
        body,
        mesh=mesh,
        in_specs=(P("band", "fft", None),),
        out_specs=(P("band", "fft", None), P(None, "fft", None)),
        check_vma=False,
    )
```

```python
import functools
import math

import jax
import jax.numpy as jnp
import ml_dtypes
import numpy as np
from jax import lax
from jax.experimental import pallas as pl
from jax.experimental.pallas import tpu as pltpu
from jax.sharding import PartitionSpec as P

GRID = 64
LANES = 128
PLANES = 8
HALF = 32
SPACING = 0.367
MIXING = 0.25
MESH = pl.DeviceIdType.MESH
BF16 = jnp.bfloat16
F32 = jnp.float32


def split_table(table):
    high = table.astype(ml_dtypes.bfloat16)
    low = (table - high.astype(np.float64)).astype(ml_dtypes.bfloat16)
    return high, low


def make_tables():
    counter = np.arange(GRID)
    angles = (counter[:, None] * counter[None, :] % GRID) * (2.0 * np.pi / GRID)
    cosine, sine = np.cos(angles), np.sin(angles)
    depth = []
    for sign in (1.0, -1.0):
        table = np.block([[cosine, -sign * sine], [sign * sine, cosine]])
        high, low = split_table(table)
        row = np.concatenate([high, low], 1)
        depth.append(np.concatenate([row, row], 0))
    order = np.concatenate([np.arange(0, GRID, 2), np.arange(1, GRID, 2)])

    def stacked(rows, columns):
        table = np.concatenate(
            [cosine[np.ix_(rows, columns)], sine[np.ix_(rows, columns)]], 0
        )
        high, low = split_table(table)
        return np.concatenate([high, low, high, low], 1)

    return depth + [
        stacked(counter, order),
        stacked(counter, counter),
        stacked(order, counter),
    ]


def split_values(values):
    high = values.astype(BF16)
    low = (values - high.astype(F32)).astype(BF16)
    return high, low


def along_lanes(values, table):
    high, low = split_values(values)
    both = jnp.dot(jnp.concatenate([high, low], 1), table, preferred_element_type=F32)
    return both[:, :LANES] + both[:, LANES:]


def along_rows(first, second, table, sign):
    high, low = split_values(jnp.concatenate([first, second], 1))
    stack = jnp.concatenate([high, high, low, low], 0)
    both = jnp.dot(table, stack, preferred_element_type=F32)
    outs = []
    for index in range(2):
        columns = slice(index * LANES, (index + 1) * LANES)
        cos_part, sin_part = both[:GRID, columns], both[GRID:, columns]
        outs.append(cos_part + sign * pltpu.roll(sin_part, GRID, 1))
    return outs


def loop(first, last, step):
    def advance(index, carry):
        step(index)
        return carry

    lax.fori_loop(first, last, advance, 0, unroll=last - first)


def far_first(count, step):
    half = count // 2
    loop(0, count - 1, lambda i: step(half + (1 - 2 * lax.rem(i, 2)) * ((i + 1) // 2)))


def pairs_far_first(count, step):
    half = count // 2

    def both(i):
        k = i // 2
        step(half + (1 - 2 * lax.rem(k, 2)) * ((k + 1) // 2), 1 - lax.rem(i, 2))

    loop(0, 2 * count - 1, both)


def wait_for(ref, sem):
    pltpu.make_async_copy(ref, ref, sem).wait()


def kernel(
    nf, nq,
    orb_hbm, fz_hbm, iz_hbm, fy_hbm, fx_hbm, iy_hbm,
    local_ref, window_ref,
    orb, fz, iz, fy, fx, iy,
    obuf, dbuf, ktab, wbuf, fsend, frecv, bsend, brecv, part, pbuf, hbuf, rsbuf, acc,
    in_sem, table_sem, sc_s, sc_r, ag_s, ag_r, cx_s, cx_r, f_s, f_r, b_s, b_r,
    p_s, p_r, rs_s, rs_r, ga_s, ga_r, fx_s, fx_r,
):
    band = lax.axis_index("band")
    me = lax.axis_index("fft")
    core = lax.rem(band, 2)
    chip = band // 2
    other = band + 1 - 2 * core
    second_root = nq
    root_chip = second_root // 2
    rows = 256 // nq
    columns = 2
    levels = nq // columns
    level, column = chip // columns, lax.rem(chip, columns)
    width = GRID * GRID // levels

    def chip_at(up, across):
        return lax.rem(level + up, levels) * columns + lax.rem(column + across, columns)


    barrier = pltpu.get_barrier_semaphore()

    def signal(b, f):
        pl.semaphore_signal(barrier, inc=1, device_id=(b, f), device_id_type=MESH)

    @pl.when(jnp.logical_and(core == 0, chip != 0))
    def _():
        signal(0, me)

    @pl.when(jnp.logical_and(core == 1, chip != root_chip))
    def _():
        signal(second_root, me)

    loop(1, nf, lambda step: signal(band, lax.rem(me + step, nf)))
    signal(other, me)

    loads = [pltpu.make_async_copy(orb_hbm, orb, in_sem)]
    loads += [
        pltpu.make_async_copy(source, target, table_sem.at[index])
        for index, (source, target) in enumerate(
            ((fz_hbm, fz), (iz_hbm, iz), (fy_hbm, fy), (fx_hbm, fx), (iy_hbm, iy))
        )
    ]
    for load in loads:
        load.start()
    loads[0].wait()

    extra = jnp.where(jnp.logical_or(band == 0, band == second_root), nq - 1, 0)
    pl.semaphore_wait(barrier, nf - 1 + 1 + extra)

    def span(place):
        return pl.ds(pl.multiple_of(place * width, width), width)

    def scatter(window, root, p):
        piece = span(p // columns)
        pltpu.make_async_remote_copy(
            orb.at[window, :, piece], wbuf.at[2 * root + window, :, piece],
            sc_s.at[window], sc_r.at[window],
            device_id=(2 * p + root, me), device_id_type=MESH,
        ).start()

    @pl.when(band == 0)
    def _():
        for window in range(2):
            pltpu.make_async_copy(
                orb.at[window, :, pl.ds(0, width)], wbuf.at[window, :, pl.ds(0, width)],
                sc_r.at[window],
            ).start()
            pairs_far_first(levels, lambda up, across: scatter(window, 0, chip_at(up, across)))

    @pl.when(band == second_root)
    def _():
        for window in range(2):
            pairs_far_first(levels, lambda up, across: scatter(window, 1, chip_at(up, across)))
            scatter(window, 1, chip)

    lane = lax.broadcasted_iota(jnp.int32, (GRID, LANES), 1)
    low_lane = lane < GRID
    sign = jnp.where(low_lane, 1.0, -1.0).astype(F32)

    def fold(values):
        return jnp.where(2 * values < GRID, values, values - GRID)

    kz = fold(jnp.where(low_lane, lane, lane - GRID))
    kx = fold(lax.broadcasted_iota(jnp.int32, (GRID, LANES), 0))
    base = kx * kx + kz * kz
    factor = (2.0 * math.pi / (GRID * SPACING)) ** 2
    scale = -MIXING / GRID**3

    for row in range(GRID // nf):
        ky = fold(me * (GRID // nf) + row)
        squared = base + ky * ky
        clamped = jnp.maximum(squared, 1).astype(F32)
        ktab[row] = jnp.where(
            squared > 0, (4.0 * math.pi / factor * scale) / clamped, 0.0
        )

    tile_lane, half_lane = low_lane[:PLANES], low_lane[:HALF]

    def tile(t):
        return pl.ds(pl.multiple_of(t * LANES, LANES), LANES)

    def pack_orbitals(t):
        first, second = orb[0, :, tile(t)], orb[1, :, tile(t)]
        obuf[pl.ds(t, PLANES, stride=GRID), :] = jnp.where(
            tile_lane, first, pltpu.roll(second, GRID, 1)
        )
        obuf[pl.ds(t + HALF, PLANES, stride=GRID), :] = jnp.where(
            tile_lane, pltpu.roll(first, GRID, 1), second
        )

    loop(0, HALF, pack_orbitals)
    for load in loads[1:]:
        load.wait()

    def gather(window):
        mine = wbuf.at[2 * core + window, :, span(level)]
        wait_for(wbuf.at[window, :, pl.ds(0, width)], sc_r.at[window])

        def send(step):
            p = lax.rem(level + step, levels) * columns + column
            pltpu.make_async_remote_copy(
                mine, mine, ag_s.at[window], ag_r.at[window],
                device_id=(2 * p + core, me), device_id_type=MESH,
            ).start()

        far_first(levels, send)

    def cross(window):
        wait_for(wbuf.at[window, :, pl.ds(0, (levels - 1) * width)], ag_r.at[window])
        whole = wbuf.at[2 * core + window]
        pltpu.make_async_remote_copy(
            whole, whole, cx_s.at[window], cx_r.at[window],
            device_id=(other, me), device_id_type=MESH,
        ).start()

    block = GRID * PLANES // nf

    def exchange(source, target, send_sem, recv_sem, k):
        if k >= 2:
            wait_for(target.at[k - 2, pl.ds(0, nf - 1)], send_sem.at[k - 2])
        own = pl.ds(pl.multiple_of(me * block, block), block)
        pltpu.make_async_copy(source.at[k, own, :], target.at[k, me], recv_sem.at[k]).start()

        def send(step):
            p = lax.rem(me + step, nf)
            pltpu.make_async_remote_copy(
                source.at[k, pl.ds(pl.multiple_of(p * block, block), block), :],
                target.at[k, me], send_sem.at[k], recv_sem.at[k],
                device_id=(band, p), device_id_type=MESH,
            ).start()

        loop(1, nf, send)

    def forward(k):
        j = (2 * core if k % 2 == 0 else 2 - 2 * core) + k // 2

        def widen(t):
            values = wbuf[j, :, tile(t)]
            turned = pltpu.roll(values, GRID, 1)
            dbuf[k, pl.ds(t, PLANES, stride=GRID), :] = jnp.where(tile_lane, values, turned)
            dbuf[k, pl.ds(t + HALF, PLANES, stride=GRID), :] = jnp.where(
                tile_lane, turned, values
            )

        loop(0, HALF, widen)

        def step(i):
            both = pl.ds(pl.multiple_of(i * 2 * GRID, 2 * GRID), 2 * GRID)
            field = along_lanes(obuf[both, :] * dbuf[k, both, :], fz[...])
            outs = along_rows(field[:GRID], field[GRID:], fy[...], sign)
            for inner in range(2):
                fsend[k, pl.ds(2 * i + inner, GRID, stride=PLANES), :] = outs[inner]

        loop(0, PLANES // 2, step)
        exchange(fsend, frecv, f_s, f_r, k)

    def middle(k):
        wait_for(frecv.at[k], f_r.at[k])

        def step(i):
            pair = []
            for inner in range(2):
                start = pl.multiple_of((2 * i + inner) * PLANES, PLANES)
                pair.append(frecv[k, :, pl.ds(start, PLANES), :].reshape(GRID, LANES))
            outs = along_rows(pair[0], pair[1], fx[...], sign)
            outs = [outs[inner] * ktab[2 * i + inner] for inner in range(2)]
            outs = along_rows(outs[0], outs[1], fx[...], -sign)
            for inner in range(2):
                bsend[k, pl.ds(2 * i + inner, GRID, stride=PLANES), :] = outs[inner]

        loop(0, GRID // nf // 2, step)
        exchange(bsend, brecv, b_s, b_r, k)

    def backward(k):
        wait_for(brecv.at[k], b_r.at[k])

        def step(i):
            pair = []
            for inner in range(2):
                start = pl.multiple_of((2 * i + inner) * PLANES, PLANES)
                pair.append(brecv[k, :, pl.ds(start, PLANES), :].reshape(GRID, LANES))
            outs = along_rows(pair[0], pair[1], iy[...], -sign)
            potential = along_lanes(jnp.concatenate(outs, 0), iz[...])
            both = pl.ds(pl.multiple_of(i * 2 * GRID, 2 * GRID), 2 * GRID)
            term = dbuf[k, both, :] * potential
            if k == 0:
                acc[both, :] = term
            else:
                acc[both, :] += term
            product = obuf[both, :] * potential
            total = product + pltpu.roll(product, GRID, 1)
            for inner in range(2):
                start = inner * GRID
                part[k, pl.ds(2 * i + inner, HALF, stride=PLANES), :] = jnp.where(
                    half_lane, total[start:start + HALF], total[start + HALF:start + GRID]
                )

        loop(0, PLANES // 2, step)

    own_piece = pl.ds(pl.multiple_of(chip * rows, rows), rows)

    def to_partner(source, target, send_sem, recv_sem):
        pltpu.make_async_remote_copy(
            source, target, send_sem, recv_sem, device_id=(other, me), device_id_type=MESH
        ).start()

    def scatter_sum(k):
        wait_for(pbuf.at[k], p_r.at[k])
        hbuf[k] = part[2 * k + 1] + pbuf[k]
        rsbuf[k, chip] = hbuf[k, own_piece, :]

        def send(up, across):
            p = chip_at(up, across)
            pltpu.make_async_remote_copy(
                hbuf.at[k, pl.ds(pl.multiple_of(p * rows, rows), rows), :], rsbuf.at[k, chip],
                rs_s.at[k], rs_r.at[k], device_id=(2 * p + core, me), device_id_type=MESH,
            ).start()

        pairs_far_first(levels, send)

    theirs = 2 - 2 * core
    share = rows * LANES // PLANES

    def gather_sum(k):
        wait_for(rsbuf.at[k, pl.ds(0, nq - 1)], rs_r.at[k])
        total = rsbuf[k, 0]
        for slot in range(1, nq):
            total = total + rsbuf[k, slot]
        for index in range(rows // PLANES):
            start = pl.multiple_of(chip * share + index * LANES, LANES)
            window_ref[theirs + k, :, pl.ds(start, LANES)] = total[index * PLANES:(index + 1) * PLANES]
        mine = window_ref.at[theirs + k, :, pl.ds(pl.multiple_of(chip * share, share), share)]

        def send(up, across):
            p = chip_at(up, across)
            pltpu.make_async_remote_copy(
                mine, mine,
                ga_s.at[k], ga_r.at[k], device_id=(2 * p + core, me), device_id_type=MESH,
            ).start()

        pairs_far_first(levels, send)

    def share_sum(k):
        wait_for(window_ref.at[k, :, pl.ds(0, (nq - 1) * share)], ga_r.at[k])
        to_partner(window_ref.at[theirs + k], window_ref.at[theirs + k], fx_s.at[k], fx_r.at[k])

    gather(0)
    gather(1)
    for window in range(2):
        cross(window)
        forward(2 * window)
        wait_for(wbuf.at[window], cx_r.at[window])
        if window == 1:
            middle(0)
        forward(2 * window + 1)
    for k in range(1, 4):
        middle(k)
    for k in range(2):
        backward(2 * k)
        to_partner(part.at[2 * k], pbuf.at[k], p_s.at[k], p_r.at[k])
        backward(2 * k + 1)
        scatter_sum(k)

    def unpack(t):
        even = acc[pl.ds(t, PLANES, stride=GRID), :]
        odd = acc[pl.ds(t + HALF, PLANES, stride=GRID), :]
        local_ref[0, :, tile(t)] = jnp.where(tile_lane, even, pltpu.roll(odd, GRID, 1))
        local_ref[1, :, tile(t)] = jnp.where(tile_lane, pltpu.roll(even, GRID, 1), odd)

    loop(0, HALF, unpack)
    for k in range(2):
        gather_sum(k)
    for k in range(2):
        share_sum(k)
    for k in range(2):
        wait_for(window_ref.at[k], fx_r.at[k])

    @pl.when(band == 0)
    def _():
        for window in range(2):
            sent = (nq - 1) * PLANES * width // LANES
            wait_for(fsend.at[0, pl.ds(0, sent), :], sc_s.at[window])

    @pl.when(band == second_root)
    def _():
        for window in range(2):
            sent = nq * PLANES * width // LANES
            wait_for(fsend.at[0, pl.ds(0, sent), :], sc_s.at[window])

    for window in range(2):
        wait_for(wbuf.at[window, :, pl.ds(0, (levels - 1) * width)], ag_s.at[window])
        wait_for(wbuf.at[window], cx_s.at[window])
    for k in range(2, 4):
        wait_for(frecv.at[k, pl.ds(0, nf - 1)], f_s.at[k])
        wait_for(brecv.at[k, pl.ds(0, nf - 1)], b_s.at[k])
    for k in range(2):
        wait_for(pbuf.at[k], p_s.at[k])
        wait_for(rsbuf.at[k, pl.ds(0, nq - 1)], rs_s.at[k])
        wait_for(window_ref.at[k, :, pl.ds(0, (nq - 1) * share)], ga_s.at[k])
        wait_for(window_ref.at[k], fx_s.at[k])


def body(orbitals):
    nf = lax.axis_size("fft")
    nq = lax.axis_size("band") // 2
    rows = 256 // nq
    block = GRID * PLANES // nf
    tables = [jnp.asarray(table) for table in make_tables()]
    dma, vmem = pltpu.SemaphoreType.DMA, pltpu.VMEM
    local_out, window_out = pl.pallas_call(
        functools.partial(kernel, nf, nq),
        out_shape=(
            jax.ShapeDtypeStruct((2, PLANES, GRID * GRID), F32),
            jax.ShapeDtypeStruct((4, PLANES, GRID * GRID), F32),
        ),
        in_specs=[pl.BlockSpec(memory_space=pltpu.HBM)] * 6,
        out_specs=(pl.BlockSpec(memory_space=vmem),) * 2,
        scratch_shapes=[
            vmem((2, PLANES, GRID * GRID), F32),
            vmem((256, 256), BF16),
            vmem((256, 256), BF16),
            vmem((128, 256), BF16),
            vmem((128, 256), BF16),
            vmem((128, 256), BF16),
            vmem((PLANES * GRID, LANES), F32),
            vmem((4, PLANES * GRID, LANES), F32),
            vmem((GRID // nf, GRID, LANES), F32),
            vmem((4, PLANES, GRID * GRID), F32),
            vmem((4, PLANES * GRID, LANES), F32),
            vmem((4, nf, block, LANES), F32),
            vmem((4, PLANES * GRID, LANES), F32),
            vmem((4, nf, block, LANES), F32),
            vmem((4, 256, LANES), F32),
            vmem((2, 256, LANES), F32),
            vmem((2, 256, LANES), F32),
            vmem((2, nq, rows, LANES), F32),
            vmem((PLANES * GRID, LANES), F32),
            dma, dma((5,)), dma((2,)), dma((2,)), dma((2,)), dma((2,)), dma((2,)), dma((2,)),
            dma((4,)), dma((4,)), dma((4,)), dma((4,)),
            dma((2,)), dma((2,)), dma((2,)), dma((2,)),
            dma((2,)), dma((2,)), dma((2,)), dma((2,)),
        ],
        compiler_params=pltpu.CompilerParams(
            collective_id=0, has_side_effects=True, vmem_limit_bytes=40 * 1024 * 1024
        ),
        cost_estimate=pl.CostEstimate(
            flops=6 * 4 * 2 * 512 * 256 * 256, bytes_accessed=1 << 20, transcendentals=0
        ),
    )(*[pltpu.with_memory_space_constraint(a, pltpu.HBM) for a in (orbitals, *tables)])
    return local_out, window_out


def solution(mesh):
    return jax.shard_map(
        body,
        mesh=mesh,
        in_specs=(P("band", "fft", None),),
        out_specs=(P("band", "fft", None), P(None, "fft", None)),
        check_vma=False,
    )
```

```python
import functools
import math

import jax
import jax.numpy as jnp
import ml_dtypes
import numpy as np
from jax import lax
from jax.experimental import pallas as pl
from jax.experimental.pallas import tpu as pltpu
from jax.sharding import PartitionSpec as P

GRID = 64
LANES = 128
PLANES = 8
HALF = 32
SPACING = 0.367
MIXING = 0.25
MESH = pl.DeviceIdType.MESH
BF16 = jnp.bfloat16
F32 = jnp.float32


def split_table(table):
    high = table.astype(ml_dtypes.bfloat16)
    low = (table - high.astype(np.float64)).astype(ml_dtypes.bfloat16)
    return high, low


def make_tables():
    counter = np.arange(GRID)
    angles = (counter[:, None] * counter[None, :] % GRID) * (2.0 * np.pi / GRID)
    cosine, sine = np.cos(angles), np.sin(angles)
    depth = []
    for sign in (1.0, -1.0):
        table = np.block([[cosine, -sign * sine], [sign * sine, cosine]])
        high, low = split_table(table)
        row = np.concatenate([high, low], 1)
        depth.append(np.concatenate([row, row], 0))
    order = np.concatenate([np.arange(0, GRID, 2), np.arange(1, GRID, 2)])

    def stacked(rows, columns):
        table = np.concatenate(
            [cosine[np.ix_(rows, columns)], sine[np.ix_(rows, columns)]], 0
        )
        high, low = split_table(table)
        return np.concatenate([high, low, high, low], 1)

    return depth + [
        stacked(counter, order),
        stacked(counter, counter),
        stacked(order, counter),
    ]


def split_values(values):
    high = values.astype(BF16)
    low = (values - high.astype(F32)).astype(BF16)
    return high, low


def along_lanes(values, table):
    high, low = split_values(values)
    both = jnp.dot(jnp.concatenate([high, low], 1), table, preferred_element_type=F32)
    return both[:, :LANES] + both[:, LANES:]


def along_rows(first, second, table, sign):
    high, low = split_values(jnp.concatenate([first, second], 1))
    stack = jnp.concatenate([high, high, low, low], 0)
    both = jnp.dot(table, stack, preferred_element_type=F32)
    outs = []
    for index in range(2):
        columns = slice(index * LANES, (index + 1) * LANES)
        cos_part, sin_part = both[:GRID, columns], both[GRID:, columns]
        outs.append(cos_part + sign * pltpu.roll(sin_part, GRID, 1))
    return outs


def loop(first, last, step):
    def advance(index, carry):
        step(index)
        return carry

    lax.fori_loop(first, last, advance, 0, unroll=last - first)


def far_first(count, step):
    half = count // 2
    loop(0, count - 1, lambda i: step(half + (1 - 2 * lax.rem(i, 2)) * ((i + 1) // 2)))


def pairs_far_first(count, step):
    half = count // 2

    def both(i):
        k = i // 2
        step(half + (1 - 2 * lax.rem(k, 2)) * ((k + 1) // 2), 1 - lax.rem(i, 2))

    loop(0, 2 * count - 1, both)


def wait_for(ref, sem):
    pltpu.make_async_copy(ref, ref, sem).wait()


def kernel(
    nf, nq,
    orb_hbm, fz_hbm, iz_hbm, fy_hbm, fx_hbm, iy_hbm,
    local_ref, window_ref,
    orb, fz, iz, fy, fx, iy,
    obuf, dbuf, ktab, wbuf, fsend, frecv, bsend, brecv, part, pbuf, hbuf, rsbuf, acc,
    in_sem, table_sem, sc_s, sc_r, ag_s, ag_r, cx_s, cx_r, f_s, f_r, b_s, b_r,
    p_s, p_r, rs_s, rs_r, ga_s, ga_r, fx_s, fx_r,
):
    band = lax.axis_index("band")
    me = lax.axis_index("fft")
    core = lax.rem(band, 2)
    chip = band // 2
    other = band + 1 - 2 * core
    second_root = nq
    root_chip = second_root // 2
    rows = 256 // nq
    columns = 2
    levels = nq // columns
    level, column = chip // columns, lax.rem(chip, columns)
    width = GRID * GRID // levels

    def chip_at(up, across):
        return lax.rem(level + up, levels) * columns + lax.rem(column + across, columns)


    barrier = pltpu.get_barrier_semaphore()

    def signal(b, f):
        pl.semaphore_signal(barrier, inc=1, device_id=(b, f), device_id_type=MESH)

    @pl.when(jnp.logical_and(core == 0, chip != 0))
    def _():
        signal(0, me)

    @pl.when(jnp.logical_and(core == 1, chip != root_chip))
    def _():
        signal(second_root, me)

    loop(1, nf, lambda step: signal(band, lax.rem(me + step, nf)))
    signal(other, me)

    loads = [pltpu.make_async_copy(orb_hbm, orb, in_sem)]
    loads += [
        pltpu.make_async_copy(source, target, table_sem.at[index])
        for index, (source, target) in enumerate(
            ((fz_hbm, fz), (iz_hbm, iz), (fy_hbm, fy), (fx_hbm, fx), (iy_hbm, iy))
        )
    ]
    for load in loads:
        load.start()
    loads[0].wait()

    extra = jnp.where(jnp.logical_or(band == 0, band == second_root), nq - 1, 0)
    pl.semaphore_wait(barrier, nf - 1 + 1 + extra)

    def span(place):
        return pl.ds(pl.multiple_of(place * width, width), width)

    def scatter(window, root, p):
        piece = span(p // columns)
        pltpu.make_async_remote_copy(
            orb.at[window, :, piece], wbuf.at[2 * root + window, :, piece],
            sc_s.at[window], sc_r.at[window],
            device_id=(2 * p + root, me), device_id_type=MESH,
        ).start()

    @pl.when(band == 0)
    def _():
        for window in range(2):
            pltpu.make_async_copy(
                orb.at[window, :, pl.ds(0, width)], wbuf.at[window, :, pl.ds(0, width)],
                sc_r.at[window],
            ).start()
            pairs_far_first(levels, lambda up, across: scatter(window, 0, chip_at(up, across)))

    @pl.when(band == second_root)
    def _():
        for window in range(2):
            pairs_far_first(levels, lambda up, across: scatter(window, 1, chip_at(up, across)))
            scatter(window, 1, chip)

    lane = lax.broadcasted_iota(jnp.int32, (GRID, LANES), 1)
    low_lane = lane < GRID
    sign = jnp.where(low_lane, 1.0, -1.0).astype(F32)

    def fold(values):
        return jnp.where(2 * values < GRID, values, values - GRID)

    kz = fold(jnp.where(low_lane, lane, lane - GRID))
    kx = fold(lax.broadcasted_iota(jnp.int32, (GRID, LANES), 0))
    base = kx * kx + kz * kz
    factor = (2.0 * math.pi / (GRID * SPACING)) ** 2
    scale = -MIXING / GRID**3

    for row in range(GRID // nf):
        ky = fold(me * (GRID // nf) + row)
        squared = base + ky * ky
        clamped = jnp.maximum(squared, 1).astype(F32)
        ktab[row] = jnp.where(
            squared > 0, (4.0 * math.pi / factor * scale) / clamped, 0.0
        )

    tile_lane, half_lane = low_lane[:PLANES], low_lane[:HALF]

    def tile(t):
        return pl.ds(pl.multiple_of(t * LANES, LANES), LANES)

    def pack_orbitals(t):
        first, second = orb[0, :, tile(t)], orb[1, :, tile(t)]
        obuf[pl.ds(t, PLANES, stride=GRID), :] = jnp.where(
            tile_lane, first, pltpu.roll(second, GRID, 1)
        )
        obuf[pl.ds(t + HALF, PLANES, stride=GRID), :] = jnp.where(
            tile_lane, pltpu.roll(first, GRID, 1), second
        )

    loop(0, HALF, pack_orbitals)
    for load in loads[1:]:
        load.wait()

    def gather(window):
        mine = wbuf.at[2 * core + window, :, span(level)]
        wait_for(wbuf.at[window, :, pl.ds(0, width)], sc_r.at[window])

        def send(step):
            p = lax.rem(level + step, levels) * columns + column
            pltpu.make_async_remote_copy(
                mine, mine, ag_s.at[window], ag_r.at[window],
                device_id=(2 * p + core, me), device_id_type=MESH,
            ).start()

        far_first(levels, send)

    def cross(window):
        wait_for(wbuf.at[window, :, pl.ds(0, (levels - 1) * width)], ag_r.at[window])
        whole = wbuf.at[2 * core + window]
        pltpu.make_async_remote_copy(
            whole, whole, cx_s.at[window], cx_r.at[window],
            device_id=(other, me), device_id_type=MESH,
        ).start()

    block = GRID * PLANES // nf

    def exchange(source, target, send_sem, recv_sem, k):
        if k >= 2:
            wait_for(target.at[k - 2, pl.ds(0, nf - 1)], send_sem.at[k - 2])
        own = pl.ds(pl.multiple_of(me * block, block), block)
        pltpu.make_async_copy(source.at[k, own, :], target.at[k, me], recv_sem.at[k]).start()

        def send(step):
            p = lax.rem(me + step, nf)
            pltpu.make_async_remote_copy(
                source.at[k, pl.ds(pl.multiple_of(p * block, block), block), :],
                target.at[k, me], send_sem.at[k], recv_sem.at[k],
                device_id=(band, p), device_id_type=MESH,
            ).start()

        loop(1, nf, send)

    def forward(k):
        j = (2 * core if k % 2 == 0 else 2 - 2 * core) + k // 2

        def widen(t):
            values = wbuf[j, :, tile(t)]
            turned = pltpu.roll(values, GRID, 1)
            dbuf[k, pl.ds(t, PLANES, stride=GRID), :] = jnp.where(tile_lane, values, turned)
            dbuf[k, pl.ds(t + HALF, PLANES, stride=GRID), :] = jnp.where(
                tile_lane, turned, values
            )

        loop(0, HALF, widen)

        def step(i):
            both = pl.ds(pl.multiple_of(i * 2 * GRID, 2 * GRID), 2 * GRID)
            field = along_lanes(obuf[both, :] * dbuf[k, both, :], fz[...])
            outs = along_rows(field[:GRID], field[GRID:], fy[...], sign)
            for inner in range(2):
                fsend[k, pl.ds(2 * i + inner, GRID, stride=PLANES), :] = outs[inner]

        loop(0, PLANES // 2, step)
        exchange(fsend, frecv, f_s, f_r, k)

    def middle(k):
        wait_for(frecv.at[k], f_r.at[k])

        def step(i):
            pair = []
            for inner in range(2):
                start = pl.multiple_of((2 * i + inner) * PLANES, PLANES)
                pair.append(frecv[k, :, pl.ds(start, PLANES), :].reshape(GRID, LANES))
            outs = along_rows(pair[0], pair[1], fx[...], sign)
            outs = [outs[inner] * ktab[2 * i + inner] for inner in range(2)]
            outs = along_rows(outs[0], outs[1], fx[...], -sign)
            for inner in range(2):
                bsend[k, pl.ds(2 * i + inner, GRID, stride=PLANES), :] = outs[inner]

        loop(0, GRID // nf // 2, step)
        exchange(bsend, brecv, b_s, b_r, k)

    def backward(k):
        wait_for(brecv.at[k], b_r.at[k])

        def step(i):
            pair = []
            for inner in range(2):
                start = pl.multiple_of((2 * i + inner) * PLANES, PLANES)
                pair.append(brecv[k, :, pl.ds(start, PLANES), :].reshape(GRID, LANES))
            outs = along_rows(pair[0], pair[1], iy[...], -sign)
            potential = along_lanes(jnp.concatenate(outs, 0), iz[...])
            both = pl.ds(pl.multiple_of(i * 2 * GRID, 2 * GRID), 2 * GRID)
            term = dbuf[k, both, :] * potential
            if k == 0:
                acc[both, :] = term
            else:
                acc[both, :] += term
            product = obuf[both, :] * potential
            total = product + pltpu.roll(product, GRID, 1)
            for inner in range(2):
                start = inner * GRID
                part[k, pl.ds(2 * i + inner, HALF, stride=PLANES), :] = jnp.where(
                    half_lane, total[start:start + HALF], total[start + HALF:start + GRID]
                )

        loop(0, PLANES // 2, step)

    own_piece = pl.ds(pl.multiple_of(chip * rows, rows), rows)

    def to_partner(source, target, send_sem, recv_sem):
        pltpu.make_async_remote_copy(
            source, target, send_sem, recv_sem, device_id=(other, me), device_id_type=MESH
        ).start()

    def scatter_sum(k):
        wait_for(pbuf.at[k], p_r.at[k])
        hbuf[k] = part[2 * k + 1] + pbuf[k]
        rsbuf[k, chip] = hbuf[k, own_piece, :]

        def send(up, across):
            p = chip_at(up, across)
            pltpu.make_async_remote_copy(
                hbuf.at[k, pl.ds(pl.multiple_of(p * rows, rows), rows), :], rsbuf.at[k, chip],
                rs_s.at[k], rs_r.at[k], device_id=(2 * p + core, me), device_id_type=MESH,
            ).start()

        pairs_far_first(levels, send)

    theirs = 2 - 2 * core
    share = rows * LANES // PLANES

    def gather_sum(k):
        wait_for(rsbuf.at[k, pl.ds(0, nq - 1)], rs_r.at[k])
        total = rsbuf[k, 0]
        for slot in range(1, nq):
            total = total + rsbuf[k, slot]
        for index in range(rows // PLANES):
            start = pl.multiple_of(chip * share + index * LANES, LANES)
            window_ref[theirs + k, :, pl.ds(start, LANES)] = total[index * PLANES:(index + 1) * PLANES]
        mine = window_ref.at[theirs + k, :, pl.ds(pl.multiple_of(chip * share, share), share)]

        def send(up, across):
            p = chip_at(up, across)
            pltpu.make_async_remote_copy(
                mine, mine,
                ga_s.at[k], ga_r.at[k], device_id=(2 * p + core, me), device_id_type=MESH,
            ).start()

        pairs_far_first(levels, send)

    def share_sum(k):
        wait_for(window_ref.at[k, :, pl.ds(0, (nq - 1) * share)], ga_r.at[k])
        to_partner(window_ref.at[theirs + k], window_ref.at[theirs + k], fx_s.at[k], fx_r.at[k])

    gather(0)
    for window in range(2):
        cross(window)
        if window == 0:
            gather(1)
        forward(2 * window)
        wait_for(wbuf.at[window], cx_r.at[window])
        if window == 1:
            middle(0)
        forward(2 * window + 1)
    for k in range(1, 4):
        middle(k)
    for k in range(2):
        backward(2 * k)
        to_partner(part.at[2 * k], pbuf.at[k], p_s.at[k], p_r.at[k])
        backward(2 * k + 1)
        scatter_sum(k)

    def unpack(t):
        even = acc[pl.ds(t, PLANES, stride=GRID), :]
        odd = acc[pl.ds(t + HALF, PLANES, stride=GRID), :]
        local_ref[0, :, tile(t)] = jnp.where(tile_lane, even, pltpu.roll(odd, GRID, 1))
        local_ref[1, :, tile(t)] = jnp.where(tile_lane, pltpu.roll(even, GRID, 1), odd)

    loop(0, HALF, unpack)
    for k in range(2):
        gather_sum(k)
    for k in range(2):
        share_sum(k)
    for k in range(2):
        wait_for(window_ref.at[k], fx_r.at[k])

    @pl.when(band == 0)
    def _():
        for window in range(2):
            sent = (nq - 1) * PLANES * width // LANES
            wait_for(fsend.at[0, pl.ds(0, sent), :], sc_s.at[window])

    @pl.when(band == second_root)
    def _():
        for window in range(2):
            sent = nq * PLANES * width // LANES
            wait_for(fsend.at[0, pl.ds(0, sent), :], sc_s.at[window])

    for window in range(2):
        wait_for(wbuf.at[window, :, pl.ds(0, (levels - 1) * width)], ag_s.at[window])
        wait_for(wbuf.at[window], cx_s.at[window])
    for k in range(2, 4):
        wait_for(frecv.at[k, pl.ds(0, nf - 1)], f_s.at[k])
        wait_for(brecv.at[k, pl.ds(0, nf - 1)], b_s.at[k])
    for k in range(2):
        wait_for(pbuf.at[k], p_s.at[k])
        wait_for(rsbuf.at[k, pl.ds(0, nq - 1)], rs_s.at[k])
        wait_for(window_ref.at[k, :, pl.ds(0, (nq - 1) * share)], ga_s.at[k])
        wait_for(window_ref.at[k], fx_s.at[k])


def body(orbitals):
    nf = lax.axis_size("fft")
    nq = lax.axis_size("band") // 2
    rows = 256 // nq
    block = GRID * PLANES // nf
    tables = [jnp.asarray(table) for table in make_tables()]
    dma, vmem = pltpu.SemaphoreType.DMA, pltpu.VMEM
    local_out, window_out = pl.pallas_call(
        functools.partial(kernel, nf, nq),
        out_shape=(
            jax.ShapeDtypeStruct((2, PLANES, GRID * GRID), F32),
            jax.ShapeDtypeStruct((4, PLANES, GRID * GRID), F32),
        ),
        in_specs=[pl.BlockSpec(memory_space=pltpu.HBM)] * 6,
        out_specs=(pl.BlockSpec(memory_space=vmem),) * 2,
        scratch_shapes=[
            vmem((2, PLANES, GRID * GRID), F32),
            vmem((256, 256), BF16),
            vmem((256, 256), BF16),
            vmem((128, 256), BF16),
            vmem((128, 256), BF16),
            vmem((128, 256), BF16),
            vmem((PLANES * GRID, LANES), F32),
            vmem((4, PLANES * GRID, LANES), F32),
            vmem((GRID // nf, GRID, LANES), F32),
            vmem((4, PLANES, GRID * GRID), F32),
            vmem((4, PLANES * GRID, LANES), F32),
            vmem((4, nf, block, LANES), F32),
            vmem((4, PLANES * GRID, LANES), F32),
            vmem((4, nf, block, LANES), F32),
            vmem((4, 256, LANES), F32),
            vmem((2, 256, LANES), F32),
            vmem((2, 256, LANES), F32),
            vmem((2, nq, rows, LANES), F32),
            vmem((PLANES * GRID, LANES), F32),
            dma, dma((5,)), dma((2,)), dma((2,)), dma((2,)), dma((2,)), dma((2,)), dma((2,)),
            dma((4,)), dma((4,)), dma((4,)), dma((4,)),
            dma((2,)), dma((2,)), dma((2,)), dma((2,)),
            dma((2,)), dma((2,)), dma((2,)), dma((2,)),
        ],
        compiler_params=pltpu.CompilerParams(
            collective_id=0, has_side_effects=True, vmem_limit_bytes=40 * 1024 * 1024
        ),
        cost_estimate=pl.CostEstimate(
            flops=6 * 4 * 2 * 512 * 256 * 256, bytes_accessed=1 << 20, transcendentals=0
        ),
    )(*[pltpu.with_memory_space_constraint(a, pltpu.HBM) for a in (orbitals, *tables)])
    return local_out, window_out


def solution(mesh):
    return jax.shard_map(
        body,
        mesh=mesh,
        in_specs=(P("band", "fft", None),),
        out_specs=(P("band", "fft", None), P(None, "fft", None)),
        check_vma=False,
    )
```

```python
import functools
import math

import jax
import jax.numpy as jnp
import ml_dtypes
import numpy as np
from jax import lax
from jax.experimental import pallas as pl
from jax.experimental.pallas import tpu as pltpu
from jax.sharding import PartitionSpec as P

GRID = 64
LANES = 128
PLANES = 8
HALF = 32
SPACING = 0.367
MIXING = 0.25
MESH = pl.DeviceIdType.MESH
BF16 = jnp.bfloat16
F32 = jnp.float32


def split_table(table):
    high = table.astype(ml_dtypes.bfloat16)
    low = (table - high.astype(np.float64)).astype(ml_dtypes.bfloat16)
    return high, low


def make_tables():
    counter = np.arange(GRID)
    angles = (counter[:, None] * counter[None, :] % GRID) * (2.0 * np.pi / GRID)
    cosine, sine = np.cos(angles), np.sin(angles)
    depth = []
    for sign in (1.0, -1.0):
        table = np.block([[cosine, -sign * sine], [sign * sine, cosine]])
        high, low = split_table(table)
        row = np.concatenate([high, low], 1)
        depth.append(np.concatenate([row, row], 0))
    order = np.concatenate([np.arange(0, GRID, 2), np.arange(1, GRID, 2)])

    def stacked(rows, columns):
        table = np.concatenate(
            [cosine[np.ix_(rows, columns)], sine[np.ix_(rows, columns)]], 0
        )
        high, low = split_table(table)
        return np.concatenate([high, low, high, low], 1)

    return depth + [
        stacked(counter, order),
        stacked(counter, counter),
        stacked(order, counter),
    ]


def split_values(values):
    high = values.astype(BF16)
    low = (values - high.astype(F32)).astype(BF16)
    return high, low


def along_lanes(values, table):
    high, low = split_values(values)
    both = jnp.dot(jnp.concatenate([high, low], 1), table, preferred_element_type=F32)
    return both[:, :LANES] + both[:, LANES:]


def along_rows(first, second, table, sign):
    high, low = split_values(jnp.concatenate([first, second], 1))
    stack = jnp.concatenate([high, high, low, low], 0)
    both = jnp.dot(table, stack, preferred_element_type=F32)
    outs = []
    for index in range(2):
        columns = slice(index * LANES, (index + 1) * LANES)
        cos_part, sin_part = both[:GRID, columns], both[GRID:, columns]
        outs.append(cos_part + sign * pltpu.roll(sin_part, GRID, 1))
    return outs


def loop(first, last, step):
    def advance(index, carry):
        step(index)
        return carry

    lax.fori_loop(first, last, advance, 0, unroll=last - first)


def far_first(count, step):
    half = count // 2
    loop(0, count - 1, lambda i: step(half + (1 - 2 * lax.rem(i, 2)) * ((i + 1) // 2)))


def pairs_far_first(count, step):
    half = count // 2

    def both(i):
        k = i // 2
        step(half + (1 - 2 * lax.rem(k, 2)) * ((k + 1) // 2), 1 - lax.rem(i, 2))

    loop(0, 2 * count - 1, both)


def wait_for(ref, sem):
    pltpu.make_async_copy(ref, ref, sem).wait()


def kernel(
    nf, nq,
    orb_hbm, fz_hbm, iz_hbm, fy_hbm, fx_hbm, iy_hbm,
    local_ref, window_ref,
    orb, fz, iz, fy, fx, iy,
    obuf, dbuf, ktab, wbuf, fsend, frecv, bsend, brecv, part, pbuf, hbuf, rsbuf, acc,
    in_sem, table_sem, sc_s, sc_r, ag_s, ag_r, cx_s, cx_r, f_s, f_r, b_s, b_r,
    p_s, p_r, rs_s, rs_r, ga_s, ga_r, fx_s, fx_r,
):
    band = lax.axis_index("band")
    me = lax.axis_index("fft")
    core = lax.rem(band, 2)
    chip = band // 2
    other = band + 1 - 2 * core
    second_root = nq
    root_chip = second_root // 2
    rows = 256 // nq
    columns = 2
    levels = nq // columns
    level, column = chip // columns, lax.rem(chip, columns)
    width = GRID * GRID // levels

    def chip_at(up, across):
        return lax.rem(level + up, levels) * columns + lax.rem(column + across, columns)


    barrier = pltpu.get_barrier_semaphore()

    def signal(b, f):
        pl.semaphore_signal(barrier, inc=1, device_id=(b, f), device_id_type=MESH)

    @pl.when(jnp.logical_and(core == 0, chip != 0))
    def _():
        signal(0, me)

    @pl.when(jnp.logical_and(core == 1, chip != root_chip))
    def _():
        signal(second_root, me)

    loop(1, nf, lambda step: signal(band, lax.rem(me + step, nf)))
    signal(other, me)

    loads = [pltpu.make_async_copy(orb_hbm, orb, in_sem)]
    loads += [
        pltpu.make_async_copy(source, target, table_sem.at[index])
        for index, (source, target) in enumerate(
            ((fz_hbm, fz), (iz_hbm, iz), (fy_hbm, fy), (fx_hbm, fx), (iy_hbm, iy))
        )
    ]
    for load in loads:
        load.start()
    loads[0].wait()

    extra = jnp.where(jnp.logical_or(band == 0, band == second_root), nq - 1, 0)
    pl.semaphore_wait(barrier, nf - 1 + 1 + extra)

    def span(place):
        return pl.ds(pl.multiple_of(place * width, width), width)

    def scatter(window, root, p):
        piece = span(p // columns)
        pltpu.make_async_remote_copy(
            orb.at[window, :, piece], wbuf.at[2 * root + window, :, piece],
            sc_s.at[window], sc_r.at[window],
            device_id=(2 * p + root, me), device_id_type=MESH,
        ).start()

    @pl.when(band == 0)
    def _():
        for window in range(2):
            pltpu.make_async_copy(
                orb.at[window, :, pl.ds(0, width)], wbuf.at[window, :, pl.ds(0, width)],
                sc_r.at[window],
            ).start()
            pairs_far_first(levels, lambda up, across: scatter(window, 0, chip_at(up, across)))

    @pl.when(band == second_root)
    def _():
        for window in range(2):
            pairs_far_first(levels, lambda up, across: scatter(window, 1, chip_at(up, across)))
            scatter(window, 1, chip)

    lane = lax.broadcasted_iota(jnp.int32, (GRID, LANES), 1)
    low_lane = lane < GRID
    sign = jnp.where(low_lane, 1.0, -1.0).astype(F32)

    def fold(values):
        return jnp.where(2 * values < GRID, values, values - GRID)

    kz = fold(jnp.where(low_lane, lane, lane - GRID))
    kx = fold(lax.broadcasted_iota(jnp.int32, (GRID, LANES), 0))
    base = kx * kx + kz * kz
    factor = (2.0 * math.pi / (GRID * SPACING)) ** 2
    scale = -MIXING / GRID**3

    for row in range(GRID // nf):
        ky = fold(me * (GRID // nf) + row)
        squared = base + ky * ky
        clamped = jnp.maximum(squared, 1).astype(F32)
        ktab[row] = jnp.where(
            squared > 0, (4.0 * math.pi / factor * scale) / clamped, 0.0
        )

    tile_lane, half_lane = low_lane[:PLANES], low_lane[:HALF]

    def tile(t):
        return pl.ds(pl.multiple_of(t * LANES, LANES), LANES)

    def pack_orbitals(t):
        first, second = orb[0, :, tile(t)], orb[1, :, tile(t)]
        obuf[pl.ds(t, PLANES, stride=GRID), :] = jnp.where(
            tile_lane, first, pltpu.roll(second, GRID, 1)
        )
        obuf[pl.ds(t + HALF, PLANES, stride=GRID), :] = jnp.where(
            tile_lane, pltpu.roll(first, GRID, 1), second
        )

    loop(0, HALF, pack_orbitals)
    for load in loads[1:]:
        load.wait()

    def gather(window):
        mine = wbuf.at[2 * core + window, :, span(level)]
        wait_for(wbuf.at[window, :, pl.ds(0, width)], sc_r.at[window])

        def send(step):
            p = lax.rem(level + step, levels) * columns + column
            pltpu.make_async_remote_copy(
                mine, mine, ag_s.at[window], ag_r.at[window],
                device_id=(2 * p + core, me), device_id_type=MESH,
            ).start()

        far_first(levels, send)

    def cross(window):
        wait_for(wbuf.at[window, :, pl.ds(0, (levels - 1) * width)], ag_r.at[window])
        whole = wbuf.at[2 * core + window]
        pltpu.make_async_remote_copy(
            whole, whole, cx_s.at[window], cx_r.at[window],
            device_id=(other, me), device_id_type=MESH,
        ).start()

    block = GRID * PLANES // nf

    def exchange(source, target, send_sem, recv_sem, k):
        if k >= 2:
            wait_for(target.at[k - 2, pl.ds(0, nf - 1)], send_sem.at[k - 2])
        own = pl.ds(pl.multiple_of(me * block, block), block)

        def send(up, across):
            p = lax.rem(me // 4 + across, 2) * 4 + lax.rem(lax.rem(me, 4) + up, 4)
            pltpu.make_async_remote_copy(
                source.at[k, pl.ds(pl.multiple_of(p * block, block), block), :],
                target.at[k, me], send_sem.at[k], recv_sem.at[k],
                device_id=(band, p), device_id_type=MESH,
            ).start()

        pairs_far_first(4, send)
        pltpu.make_async_copy(source.at[k, own, :], target.at[k, me], recv_sem.at[k]).start()

    def forward(k):
        j = (2 * core if k % 2 == 0 else 2 - 2 * core) + k // 2

        def widen(t):
            values = wbuf[j, :, tile(t)]
            turned = pltpu.roll(values, GRID, 1)
            dbuf[k, pl.ds(t, PLANES, stride=GRID), :] = jnp.where(tile_lane, values, turned)
            dbuf[k, pl.ds(t + HALF, PLANES, stride=GRID), :] = jnp.where(
                tile_lane, turned, values
            )

        loop(0, HALF, widen)

        def step(i):
            both = pl.ds(pl.multiple_of(i * 2 * GRID, 2 * GRID), 2 * GRID)
            field = along_lanes(obuf[both, :] * dbuf[k, both, :], fz[...])
            outs = along_rows(field[:GRID], field[GRID:], fy[...], sign)
            for inner in range(2):
                fsend[k, pl.ds(2 * i + inner, GRID, stride=PLANES), :] = outs[inner]

        loop(0, PLANES // 2, step)
        exchange(fsend, frecv, f_s, f_r, k)

    def middle(k):
        wait_for(frecv.at[k], f_r.at[k])

        def step(i):
            pair = []
            for inner in range(2):
                start = pl.multiple_of((2 * i + inner) * PLANES, PLANES)
                pair.append(frecv[k, :, pl.ds(start, PLANES), :].reshape(GRID, LANES))
            outs = along_rows(pair[0], pair[1], fx[...], sign)
            outs = [outs[inner] * ktab[2 * i + inner] for inner in range(2)]
            outs = along_rows(outs[0], outs[1], fx[...], -sign)
            for inner in range(2):
                bsend[k, pl.ds(2 * i + inner, GRID, stride=PLANES), :] = outs[inner]

        loop(0, GRID // nf // 2, step)
        exchange(bsend, brecv, b_s, b_r, k)

    def backward(k):
        wait_for(brecv.at[k], b_r.at[k])

        def step(i):
            pair = []
            for inner in range(2):
                start = pl.multiple_of((2 * i + inner) * PLANES, PLANES)
                pair.append(brecv[k, :, pl.ds(start, PLANES), :].reshape(GRID, LANES))
            outs = along_rows(pair[0], pair[1], iy[...], -sign)
            potential = along_lanes(jnp.concatenate(outs, 0), iz[...])
            both = pl.ds(pl.multiple_of(i * 2 * GRID, 2 * GRID), 2 * GRID)
            term = dbuf[k, both, :] * potential
            if k == 0:
                acc[both, :] = term
            else:
                acc[both, :] += term
            product = obuf[both, :] * potential
            total = product + pltpu.roll(product, GRID, 1)
            for inner in range(2):
                start = inner * GRID
                part[k, pl.ds(2 * i + inner, HALF, stride=PLANES), :] = jnp.where(
                    half_lane, total[start:start + HALF], total[start + HALF:start + GRID]
                )

        loop(0, PLANES // 2, step)

    own_piece = pl.ds(pl.multiple_of(chip * rows, rows), rows)

    def to_partner(source, target, send_sem, recv_sem):
        pltpu.make_async_remote_copy(
            source, target, send_sem, recv_sem, device_id=(other, me), device_id_type=MESH
        ).start()

    def scatter_sum(k):
        wait_for(pbuf.at[k], p_r.at[k])
        hbuf[k] = part[2 * k + 1] + pbuf[k]
        rsbuf[k, chip] = hbuf[k, own_piece, :]

        def send(up, across):
            p = chip_at(up, across)
            pltpu.make_async_remote_copy(
                hbuf.at[k, pl.ds(pl.multiple_of(p * rows, rows), rows), :], rsbuf.at[k, chip],
                rs_s.at[k], rs_r.at[k], device_id=(2 * p + core, me), device_id_type=MESH,
            ).start()

        pairs_far_first(levels, send)

    theirs = 2 - 2 * core
    share = rows * LANES // PLANES

    def gather_sum(k):
        wait_for(rsbuf.at[k, pl.ds(0, nq - 1)], rs_r.at[k])
        total = rsbuf[k, 0]
        for slot in range(1, nq):
            total = total + rsbuf[k, slot]
        for index in range(rows // PLANES):
            start = pl.multiple_of(chip * share + index * LANES, LANES)
            window_ref[theirs + k, :, pl.ds(start, LANES)] = total[index * PLANES:(index + 1) * PLANES]
        mine = window_ref.at[theirs + k, :, pl.ds(pl.multiple_of(chip * share, share), share)]

        def send(up, across):
            p = chip_at(up, across)
            pltpu.make_async_remote_copy(
                mine, mine,
                ga_s.at[k], ga_r.at[k], device_id=(2 * p + core, me), device_id_type=MESH,
            ).start()

        pairs_far_first(levels, send)

    def share_sum(k):
        wait_for(window_ref.at[k, :, pl.ds(0, (nq - 1) * share)], ga_r.at[k])
        to_partner(window_ref.at[theirs + k], window_ref.at[theirs + k], fx_s.at[k], fx_r.at[k])

    gather(0)
    for window in range(2):
        cross(window)
        if window == 0:
            gather(1)
        forward(2 * window)
        wait_for(wbuf.at[window], cx_r.at[window])
        if window == 1:
            middle(0)
        forward(2 * window + 1)
    for k in range(1, 4):
        middle(k)
    for k in range(2):
        backward(2 * k)
        to_partner(part.at[2 * k], pbuf.at[k], p_s.at[k], p_r.at[k])
        backward(2 * k + 1)
        scatter_sum(k)

    def unpack(t):
        even = acc[pl.ds(t, PLANES, stride=GRID), :]
        odd = acc[pl.ds(t + HALF, PLANES, stride=GRID), :]
        local_ref[0, :, tile(t)] = jnp.where(tile_lane, even, pltpu.roll(odd, GRID, 1))
        local_ref[1, :, tile(t)] = jnp.where(tile_lane, pltpu.roll(even, GRID, 1), odd)

    loop(0, HALF, unpack)
    for k in range(2):
        gather_sum(k)
    for k in range(2):
        share_sum(k)
    for k in range(2):
        wait_for(window_ref.at[k], fx_r.at[k])

    @pl.when(band == 0)
    def _():
        for window in range(2):
            sent = (nq - 1) * PLANES * width // LANES
            wait_for(fsend.at[0, pl.ds(0, sent), :], sc_s.at[window])

    @pl.when(band == second_root)
    def _():
        for window in range(2):
            sent = nq * PLANES * width // LANES
            wait_for(fsend.at[0, pl.ds(0, sent), :], sc_s.at[window])

    for window in range(2):
        wait_for(wbuf.at[window, :, pl.ds(0, (levels - 1) * width)], ag_s.at[window])
        wait_for(wbuf.at[window], cx_s.at[window])
    for k in range(2, 4):
        wait_for(frecv.at[k, pl.ds(0, nf - 1)], f_s.at[k])
        wait_for(brecv.at[k, pl.ds(0, nf - 1)], b_s.at[k])
    for k in range(2):
        wait_for(pbuf.at[k], p_s.at[k])
        wait_for(rsbuf.at[k, pl.ds(0, nq - 1)], rs_s.at[k])
        wait_for(window_ref.at[k, :, pl.ds(0, (nq - 1) * share)], ga_s.at[k])
        wait_for(window_ref.at[k], fx_s.at[k])


def body(orbitals):
    nf = lax.axis_size("fft")
    nq = lax.axis_size("band") // 2
    rows = 256 // nq
    block = GRID * PLANES // nf
    tables = [jnp.asarray(table) for table in make_tables()]
    dma, vmem = pltpu.SemaphoreType.DMA, pltpu.VMEM
    local_out, window_out = pl.pallas_call(
        functools.partial(kernel, nf, nq),
        out_shape=(
            jax.ShapeDtypeStruct((2, PLANES, GRID * GRID), F32),
            jax.ShapeDtypeStruct((4, PLANES, GRID * GRID), F32),
        ),
        in_specs=[pl.BlockSpec(memory_space=pltpu.HBM)] * 6,
        out_specs=(pl.BlockSpec(memory_space=vmem),) * 2,
        scratch_shapes=[
            vmem((2, PLANES, GRID * GRID), F32),
            vmem((256, 256), BF16),
            vmem((256, 256), BF16),
            vmem((128, 256), BF16),
            vmem((128, 256), BF16),
            vmem((128, 256), BF16),
            vmem((PLANES * GRID, LANES), F32),
            vmem((4, PLANES * GRID, LANES), F32),
            vmem((GRID // nf, GRID, LANES), F32),
            vmem((4, PLANES, GRID * GRID), F32),
            vmem((4, PLANES * GRID, LANES), F32),
            vmem((4, nf, block, LANES), F32),
            vmem((4, PLANES * GRID, LANES), F32),
            vmem((4, nf, block, LANES), F32),
            vmem((4, 256, LANES), F32),
            vmem((2, 256, LANES), F32),
            vmem((2, 256, LANES), F32),
            vmem((2, nq, rows, LANES), F32),
            vmem((PLANES * GRID, LANES), F32),
            dma, dma((5,)), dma((2,)), dma((2,)), dma((2,)), dma((2,)), dma((2,)), dma((2,)),
            dma((4,)), dma((4,)), dma((4,)), dma((4,)),
            dma((2,)), dma((2,)), dma((2,)), dma((2,)),
            dma((2,)), dma((2,)), dma((2,)), dma((2,)),
        ],
        compiler_params=pltpu.CompilerParams(
            collective_id=0, has_side_effects=True, vmem_limit_bytes=40 * 1024 * 1024
        ),
        cost_estimate=pl.CostEstimate(
            flops=6 * 4 * 2 * 512 * 256 * 256, bytes_accessed=1 << 20, transcendentals=0
        ),
    )(*[pltpu.with_memory_space_constraint(a, pltpu.HBM) for a in (orbitals, *tables)])
    return local_out, window_out


def solution(mesh):
    return jax.shard_map(
        body,
        mesh=mesh,
        in_specs=(P("band", "fft", None),),
        out_specs=(P("band", "fft", None), P(None, "fft", None)),
        check_vma=False,
    )
```
